128 devices in a mesh: dp: 32 (over y, z, core), mp: 4 (over x).
Axes of the slice: x: 4, y: 4, z: 4, core: 2. Of those that a mesh axis runs over, the one named last changes fastest.
Arguments:
- hidden_states: bfloat16 [32768, 8192], P('dp'), may hold values from -6 to 6
- norm_gain: float32 [8192], replicated, may hold values from 0.6 to 9
- w_query: bfloat16 [8192, 4096], P('dp', 'mp'), may hold values from -0.0625 to 0.0625
- w_keyval: bfloat16 [8192, 1024], P('dp', 'mp'), may hold values from -0.0625 to 0.0625
- query_bias: float32 [4096], P('mp'), may hold values from -3 to 3
- keyval_bias: float32 [1024], P('mp'), may hold values from -3 to 3
- group_dest: int32 [32, 16], replicated, may hold values from 0 to 31, as said below
- group_offset: int32 [32, 16], replicated, may hold values from 0 to 960, as said below
- group_length: int32 [32, 16], replicated, may hold values from 8 to 64, as said below
Outputs:
- attention_out: bfloat16 [32768, 4096], P(('dp', 'mp'))
The draws below stay inside these ranges and needn't reach their ends.
Inputs may be any that keep to these rules, and one draw needn't show every extreme that they name: `group_dest`: the 16 groups of one rollout pack go to different training packs, and every training pack receives exactly 16 groups. `group_offset`: multiples of 64; the groups that one training pack receives have different offsets. `group_length`: each value is 64, 32, 16 or 8, and each of the four occurs in every draw.
All inputs are finite; a program needn't handle non-finite values.
Results may differ from the reference program's by a relative error of at most 0.006.
The reference program's roundings to bfloat16 on the way (of `normed`, `weights` and `context`) count: a program that leaves them out, or rounds other values in their place, can miss the bound.
Values may be sent and summed in bfloat16 or wider, within the bound.
No kernel may reach another device: no remote copies, remote signals or barrier semaphores. Data moves between devices by JAX's collectives and lax.ppermute only.
A program may use at most 128 MiB of HBM per device.

```python
import jax
import jax.numpy as jnp
from jax import lax

D = 8192
HQ = 32
HK = 4
HD = 128
TOK_DEV = 1024
GROUP = 64
NPACK = 32
GROUPS = 16
TOKENS = 32768


def group_plan(key):
    key_shift, key_source, key_target, key_slots = jax.random.split(key, 4)
    shifts = jax.random.permutation(key_shift, NPACK)[:GROUPS]
    source_order = jax.random.permutation(key_source, NPACK)
    target_order = jax.random.permutation(key_target, NPACK)
    destination = target_order[(source_order[:, None] + shifts[None, :]) % NPACK]
    slot_table = jax.vmap(lambda single: jax.random.permutation(single, GROUPS))(jax.random.split(key_slots, NPACK))
    slot_index = slot_table[destination, jnp.arange(GROUPS)[None, :]]
    return (destination.astype(jnp.int32), (slot_index * GROUP).astype(jnp.int32))


def draw_group_dest(key, part):
    destination, offsets = group_plan(key)
    return destination


def draw_group_offset(key, part):
    destination, offsets = group_plan(key)
    return offsets


def draw_group_length(key, part):
    key = jax.random.fold_in(key, 5)
    key_class, key_place = jax.random.split(key)
    classes = jax.random.randint(key_class, (NPACK * GROUPS,), 0, 4)
    chosen = jax.random.permutation(key_place, NPACK * GROUPS)[:4]
    classes = classes.at[chosen].set(jnp.arange(4))
    table = jnp.array([GROUP, GROUP // 2, GROUP // 4, GROUP // 8], jnp.int32)
    return table[classes].reshape(NPACK, GROUPS)


def draw_norm_gain(key, part):
    key = jax.random.fold_in(key, 11)
    return jax.random.uniform(key, (D,), jnp.float32, 0.6, 1.4)


def steps_of(stream_key, shape, cuts, smallest, high):
    loudness, own = 1.0, jax.random.fold_in(stream_key, 6)
    for dim, parts in cuts:
        draws = jnp.exp(jax.random.uniform(jax.random.fold_in(own, dim), (parts,), jnp.float32, smallest / len(cuts), high / len(cuts)))
        loudness = loudness * jnp.repeat(draws, shape[dim] // parts).reshape([-1 if axis == dim else 1 for axis in range(len(shape))])
    return loudness


def gaussian(rng, shape, deviation, most, cuts=(), kind=jnp.bfloat16):
    drawn = jax.random.normal(rng, shape, jnp.float32) * deviation
    if len(cuts) > 0:
        drawn = steps_of(rng, shape, cuts, -0.22, 0.18) * drawn
    return jnp.clip(drawn, min=-most, max=most).astype(kind)


def setup_inputs(seed: int = 0) -> dict:
    key_list = jax.random.split(jax.random.key(seed), 10)
    hidden_states = gaussian(key_list[0], (TOKENS, D), 1.0, 6.0, ((0, 32),))
    norm_gain = draw_norm_gain(jax.random.fold_in(key_list[9], 71), 0)
    w_query = gaussian(key_list[2], (D, HQ * HD), D ** -0.5, 0.0625, ((0, 32), (1, 4)))
    w_keyval = gaussian(key_list[3], (D, HK * 2 * HD), D ** -0.5, 0.0625, ((0, 32), (1, 4)))
    query_bias = gaussian(key_list[4], (HQ * HD,), 0.5, 3.0, ((0, 4),), jnp.float32)
    keyval_bias = gaussian(key_list[5], (HK * 2 * HD,), 0.5, 3.0, ((0, 4),), jnp.float32)
    group_dest = draw_group_dest(jax.random.fold_in(key_list[9], 71), 0)
    group_offset = draw_group_offset(jax.random.fold_in(key_list[9], 71), 0)
    group_length = draw_group_length(jax.random.fold_in(key_list[9], 71), 0)
    return {"hidden_states": hidden_states, "norm_gain": norm_gain, "w_query": w_query, "w_keyval": w_keyval, "query_bias": query_bias, "keyval_bias": keyval_bias, "group_dest": group_dest, "group_offset": group_offset, "group_length": group_length}


rope_base = 1000000.0
norm_epsilon = 1e-06

def rotary(values_in, position):
    half_width = values_in.shape[-1] // 2
    frequency = rope_base ** (-(jnp.arange(half_width, dtype=jnp.float32) * 2.0) / values_in.shape[-1])
    angles = position.astype(jnp.float32)[:, None] * frequency[None, :]
    cosine = jnp.cos(angles)[:, None, :]
    sine_part = jnp.sin(angles)[:, None, :]
    first_half = values_in[..., :half_width]
    second_half = values_in[..., half_width:]
    return jnp.concatenate([first_half * cosine - second_half * sine_part, second_half * cosine + first_half * sine_part], -1)

def positions(lengths, group_rows):
    within = jnp.arange(group_rows, dtype=jnp.int32)
    return (within[None, :] % lengths[:, None]).reshape(-1)

def allowed_pairs(lengths, group_rows):
    within = jnp.arange(group_rows, dtype=jnp.int32)
    segment = within[None, :] // lengths[:, None]
    same = segment[:, :, None] == segment[:, None, :]
    causal = within[None, :] <= within[:, None]
    return same & causal[None]

def attend(query_heads, key_heads, value_heads, lengths):
    score_scale = query_heads.shape[-1] ** (-0.5)
    scores = jnp.einsum('gqhrd,gkhd->ghrqk', query_heads.astype(jnp.float32), key_heads.astype(jnp.float32)) * score_scale
    allowed = allowed_pairs(lengths, query_heads.shape[1])[:, None, None]
    scores = jnp.where(allowed, scores, -jnp.inf)
    row_max = lax.optimization_barrier(jnp.max(scores, -1, keepdims=True))
    weights = jnp.exp(scores - row_max)
    weights = (weights / lax.optimization_barrier(jnp.sum(weights, -1, keepdims=True))).astype(jnp.bfloat16)
    context = jnp.einsum('ghrqk,gkhd->gqhrd', weights.astype(jnp.float32), value_heads.astype(jnp.float32))
    return context.astype(jnp.bfloat16)

def reference(hidden_states, norm_gain, w_query, w_keyval, query_bias, keyval_bias, group_dest, group_offset, group_length):

    def one_pack(inputs):
        tokens_in, lengths = inputs
        widened = tokens_in.astype(jnp.float32)
        mean_square = lax.optimization_barrier(jnp.mean(widened * widened, -1, keepdims=True))
        normed = (widened * lax.rsqrt(mean_square + norm_epsilon) * norm_gain).astype(jnp.bfloat16)
        query = jnp.dot(normed, w_query, preferred_element_type=jnp.float32) + query_bias
        keyval = jnp.dot(normed, w_keyval, preferred_element_type=jnp.float32) + keyval_bias
        keyval = keyval.reshape(TOK_DEV, HK, 2, HD)
        position = positions(lengths, GROUP)
        query_rot = rotary(query.reshape(TOK_DEV, HQ, HD), position).astype(jnp.bfloat16)
        key_rot = rotary(keyval[:, :, 0], position).astype(jnp.bfloat16)
        value_part = keyval[:, :, 1].astype(jnp.bfloat16)
        context = attend(query_rot.reshape(GROUPS, GROUP, HK, HQ // HK, HD), key_rot.reshape(GROUPS, GROUP, HK, HD), value_part.reshape(GROUPS, GROUP, HK, HD), lengths)
        return context.reshape(GROUPS, GROUP, HQ * HD)
    packed = hidden_states.reshape(NPACK, TOK_DEV, D)
    contexts = lax.map(one_pack, (packed, group_length))
    target = (group_dest * GROUPS + group_offset // GROUP).reshape(-1).astype(jnp.int32)
    placed = jnp.zeros((NPACK * GROUPS, GROUP, HQ * HD), jnp.bfloat16)
    placed = placed.at[target].set(contexts.reshape(NPACK * GROUPS, GROUP, HQ * HD))
    return placed.reshape(TOKENS, HQ * HD)
```

```python
import jax
import jax.numpy as jnp
import numpy as np
from jax import lax
from jax.experimental import pallas as pl
from jax.experimental.pallas import tpu as pltpu
from jax.sharding import PartitionSpec as P

HD = 128
GROUP = 64
SIDE = 4
MIB = 1024 * 1024

rope_base = 1000000.0
norm_epsilon = 1e-06


def rope_tables():
    half = HD // 2
    frequency = np.float32(rope_base) ** (
        -(np.arange(half, dtype=np.float32) * np.float32(2.0)) / np.float32(HD)
    )
    within = np.arange(GROUP)
    position = np.concatenate([within % length for length in (64, 32, 16, 8)])
    angles = position.astype(np.float32)[:, None] * frequency[None, :].astype(np.float32)
    cosine, sine = np.cos(angles), np.sin(angles)
    return (
        np.concatenate([cosine, cosine], 1).astype(np.float32),
        np.concatenate([-sine, sine], 1).astype(np.float32),
    )


def device_index(y, z, core):
    return ((y % SIDE) * SIDE + (z % SIDE)) * 2 + core


def shift_pairs(first, second):
    pairs = []
    for y in range(SIDE):
        for z in range(SIDE):
            pairs.append((device_index(y, z, 0), device_index(y + first, z + second, 0)))
            pairs.append((device_index(y, z, 1), device_index(y + second, z + first, 1)))
    return pairs


def swap_pairs():
    return [
        (device_index(y, z, core), device_index(y, z, 1 - core))
        for y in range(SIDE)
        for z in range(SIDE)
        for core in range(2)
    ]


def source_table():
    table = np.zeros((32, 32), np.int32)
    for y in range(SIDE):
        for z in range(SIDE):
            for core in range(2):

                def pieces(c, second):
                    found = []
                    for first in range(SIDE):
                        if c == 0:
                            found.append(device_index(y - first, z - second, c))
                        else:
                            found.append(device_index(y - second, z - first, c))
                    return found

                other = 1 - core
                order = pieces(core, 0) + pieces(other, 0)
                order += pieces(core, 1) + pieces(core, 3) + pieces(other, 1) + pieces(other, 3)
                order += pieces(core, 2) + pieces(other, 2)
                table[device_index(y, z, core)] = order
    return table


def norm_kernel(order_ref, hidden_ref, gain_ref, early_ref, middle_ref, late_ref):
    features = hidden_ref.shape[1]
    depth = features // 32
    widened = hidden_ref[...].astype(jnp.float32)
    mean_square = jnp.sum(widened * widened, -1, keepdims=True) * (1.0 / features)
    scale = lax.rsqrt(mean_square + norm_epsilon)
    place = 0
    for ref in (early_ref, middle_ref, late_ref):
        for j in range(ref.shape[1] // depth):
            start = pl.multiple_of(order_ref[place] * depth, depth)
            block = hidden_ref[:, pl.ds(start, depth)].astype(jnp.float32)
            gain = gain_ref[:, pl.ds(start, depth)]
            ref[:, j * depth : (j + 1) * depth] = (block * scale * gain).astype(jnp.bfloat16)
            place += 1


def norm(order, hidden, gain, widths):
    rows, features = hidden.shape
    tile = 128
    return pl.pallas_call(
        norm_kernel,
        grid_spec=pltpu.PrefetchScalarGridSpec(
            num_scalar_prefetch=1,
            grid=(rows // tile,),
            in_specs=[
                pl.BlockSpec((tile, features), lambda i, order: (i, 0)),
                pl.BlockSpec((1, features), lambda i, order: (0, 0)),
            ],
            out_specs=[pl.BlockSpec((tile, w), lambda i, order: (i, 0)) for w in widths],
        ),
        out_shape=[jax.ShapeDtypeStruct((rows, w), jnp.bfloat16) for w in widths],
        compiler_params=pltpu.CompilerParams(vmem_limit_bytes=24 * MIB),
        cost_estimate=pl.CostEstimate(
            flops=6 * rows * features, bytes_accessed=4 * rows * features, transcendentals=rows
        ),
        name="norm",
    )(order, hidden, gain)


def product(x_ref, pieces):
    weights = jnp.concatenate([piece[...] for piece in pieces], axis=0)
    return jnp.dot(x_ref[...], weights, preferred_element_type=jnp.float32)


def first_kernel(x_ref, *refs):
    refs[-1][...] = product(x_ref, refs[:-1])


def add_kernel(total_ref, x_ref, *refs):
    refs[-1][...] = total_ref[...] + product(x_ref, refs[:-1])


def whole(shape):
    return pl.BlockSpec(shape, lambda i: (0,) * len(shape), pipeline_mode=pl.Buffered(1))


def matmul_cost(rows, depth, columns, more):
    return pl.CostEstimate(
        flops=2 * rows * depth * columns,
        bytes_accessed=2 * depth * (rows + columns) + 4 * more * rows * columns,
        transcendentals=0,
    )


def project(total, x, pieces):
    rows, depth = x.shape
    columns = pieces[0].shape[1]
    tile = 256
    block = pl.BlockSpec((tile, columns), lambda i: (i, 0))
    x_block = pl.BlockSpec((tile, depth), lambda i: (i, 0))
    weights = [whole(piece.shape) for piece in pieces]
    return pl.pallas_call(
        first_kernel if total is None else add_kernel,
        grid=(rows // tile,),
        in_specs=([] if total is None else [block]) + [x_block] + weights,
        out_specs=block,
        out_shape=jax.ShapeDtypeStruct((rows, columns), jnp.float32),
        input_output_aliases={} if total is None else {0: 0},
        compiler_params=pltpu.CompilerParams(vmem_limit_bytes=40 * MIB),
        cost_estimate=matmul_cost(rows, depth, columns, 1 if total is None else 2),
        name="project",
    )(*([] if total is None else [total]), x, *pieces)


def attend_kernel(
    dest_ref, length_ref, total_ref, x_ref, bias_ref, cosine_ref, sine_ref, *refs
):
    pieces, (out_ref, context, sems) = refs[:-3], refs[-3:]
    step = pl.program_id(0)
    slot = lax.rem(step, 2)
    rows, columns = total_ref.shape
    heads = columns // HD - 2
    groups = rows // GROUP

    def copies(at_step, at_slot):
        return [
            pltpu.make_async_copy(
                context.at[at_slot, pl.ds(g * GROUP, GROUP)],
                out_ref.at[dest_ref[at_step * groups + g]],
                sems.at[at_slot, g],
            )
            for g in range(groups)
        ]

    lengths = [length_ref[step * groups + g] for g in range(groups)]
    row_tables = []
    for table in (cosine_ref, sine_ref):
        parts = []
        for length in lengths:
            index = (
                (length < 64).astype(jnp.int32)
                + (length < 32).astype(jnp.int32)
                + (length < 16).astype(jnp.int32)
            )
            parts.append(table[pl.ds(pl.multiple_of(index * GROUP, GROUP), GROUP), :])
        row_tables.append(jnp.concatenate(parts, 0))
    cosine, sine = row_tables

    summed = total_ref[...] + product(x_ref, pieces) + bias_ref[...]

    def rotated(column):
        head = summed[:, column : column + HD]
        return (head * cosine + pltpu.roll(head, HD // 2, 1) * sine).astype(jnp.bfloat16)

    query = [rotated(h * HD) for h in range(heads)]
    key = rotated(heads * HD)
    value = summed[:, (heads + 1) * HD :].astype(jnp.bfloat16)

    @pl.when(step >= 2)
    def _():
        for copy in copies(step - 2, slot):
            copy.wait()

    tile = 2 * GROUP
    row = lax.broadcasted_iota(jnp.int32, (tile, tile), 0)
    column = lax.broadcasted_iota(jnp.int32, (tile, tile), 1)
    for t in range(rows // tile):
        length = jnp.where(row < GROUP, lengths[2 * t], lengths[2 * t + 1])
        allowed = (column >= (row & -length)) & (column <= row)
        span = slice(t * tile, (t + 1) * tile)
        stacked = jnp.concatenate([q[span] for q in query], 0)
        scores = lax.dot_general(
            stacked, key[span], (((1,), (1,)), ((), ())), preferred_element_type=jnp.float32
        ) * (HD ** (-0.5))
        scores = jnp.where(allowed[None], scores.reshape(heads, tile, tile), -jnp.inf)
        weights = jnp.exp(scores - jnp.max(scores, -1, keepdims=True))
        weights = weights * (1.0 / jnp.sum(weights, -1, keepdims=True))
        weights = weights.astype(jnp.bfloat16).reshape(heads * tile, tile)
        mixed = jnp.dot(weights, value[span], preferred_element_type=jnp.float32)
        mixed = mixed.astype(jnp.bfloat16)
        for h in range(heads):
            context[slot, span, h * HD : (h + 1) * HD] = mixed[h * tile : (h + 1) * tile]

    for copy in copies(step, slot):
        copy.start()

    @pl.when(step == pl.num_programs(0) - 1)
    def _():
        for copy in copies(step - 1, 1 - slot) + copies(step, slot):
            copy.wait()


def attend(dest, lengths, total, x, bias, pieces, packs):
    rows, depth = x.shape
    columns = total.shape[1]
    tile = 256
    cosine, sine = rope_tables()
    width = columns - 2 * HD

    def fixed(shape):
        return pl.BlockSpec(
            shape, lambda i, *_: (0,) * len(shape), pipeline_mode=pl.Buffered(1)
        )

    return pl.pallas_call(
        attend_kernel,
        grid_spec=pltpu.PrefetchScalarGridSpec(
            num_scalar_prefetch=2,
            grid=(rows // tile,),
            in_specs=[
                pl.BlockSpec((tile, columns), lambda i, *_: (i, 0)),
                pl.BlockSpec((tile, depth), lambda i, *_: (i, 0)),
                fixed(bias.shape),
                fixed(cosine.shape),
                fixed(sine.shape),
            ]
            + [fixed(piece.shape) for piece in pieces],
            out_specs=pl.BlockSpec(memory_space=pl.ANY),
            scratch_shapes=[
                pltpu.VMEM((2, tile, width), jnp.bfloat16),
                pltpu.SemaphoreType.DMA((2, tile // GROUP)),
            ],
        ),
        out_shape=jax.ShapeDtypeStruct((packs, GROUP, width), jnp.bfloat16),
        compiler_params=pltpu.CompilerParams(vmem_limit_bytes=48 * MIB),
        cost_estimate=matmul_cost(rows, depth, columns, 2),
        name="attend",
    )(dest, lengths, total, x, bias, cosine, sine, *pieces)


def place_kernel(source_ref, *refs):
    count = len(refs) // 2
    for given, taken in zip(refs[:count], refs[count:], strict=True):
        taken[...] = given[0]


def place(source, received, parts):
    packs, group, width = received.shape
    per_part = source.shape[0] // parts

    def given(part):
        return pl.BlockSpec(
            (1, group, width), lambda j, source: (source[part * per_part + j], 0, 0)
        )

    return pl.pallas_call(
        place_kernel,
        grid_spec=pltpu.PrefetchScalarGridSpec(
            num_scalar_prefetch=1,
            grid=(per_part,),
            in_specs=[given(part) for part in range(parts)],
            out_specs=[pl.BlockSpec((group, width), lambda j, source: (j, 0))] * parts,
        ),
        out_shape=[jax.ShapeDtypeStruct((per_part * group, width), received.dtype)] * parts,
        name="place",
    )(source, *([received] * parts))


def join_kernel(order_ref, *refs):
    width = refs[0].shape[1]
    for part, ref in enumerate(refs[:-1]):
        start = pl.multiple_of(order_ref[part] * width, width)
        refs[-1][:, pl.ds(start, width)] = ref[...]


def join(order, parts):
    rows, width = parts[0].shape
    tile = 64
    return pl.pallas_call(
        join_kernel,
        grid_spec=pltpu.PrefetchScalarGridSpec(
            num_scalar_prefetch=1,
            grid=(rows // tile,),
            in_specs=[pl.BlockSpec((tile, width), lambda i, order: (i, 0))] * len(parts),
            out_specs=pl.BlockSpec((tile, width * len(parts)), lambda i, order: (i, 0)),
        ),
        out_shape=jax.ShapeDtypeStruct((rows, width * len(parts)), parts[0].dtype),
        name="join",
    )(order, *parts)


def per_device(
    hidden_states,
    norm_gain,
    w_query,
    w_keyval,
    query_bias,
    keyval_bias,
    group_dest,
    group_offset,
    group_length,
):
    own = lax.axis_index("dp")
    plane = lax.axis_index("mp")
    planes = lax.axis_size("mp")
    packs, groups = group_dest.shape
    rows, features = hidden_states.shape

    def first(piece, by):
        return lax.ppermute(piece, "dp", shift_pairs(by, 0))

    def second(piece, by):
        return lax.ppermute(piece, "dp", shift_pairs(0, by))

    def swap(piece):
        return lax.ppermute(piece, "dp", swap_pairs())

    weights = jnp.concatenate([w_query, w_keyval], 1)
    bias = jnp.concatenate([query_bias, keyval_bias])[None]
    near = [weights, first(weights, 1), first(weights, 2), first(weights, -1)]
    ahead = [second(piece, 1) for piece in near]
    behind = [second(piece, -1) for piece in near]
    far = [second(ahead[0], 1), second(ahead[1], 1), second(behind[2], -1), second(behind[3], -1)]
    early = near + [swap(piece) for piece in near]
    middle = ahead + behind + [swap(piece) for piece in ahead + behind]
    late = far + [swap(piece) for piece in far]

    depth = weights.shape[0]
    order = lax.dynamic_index_in_dim(jnp.asarray(source_table()), own, 0, keepdims=False)
    x_early, x_middle, x_late = norm(
        order,
        hidden_states,
        norm_gain[None],
        [len(early) * depth, len(middle) * depth, len(late) * depth],
    )
    total = project(None, x_early, early)
    total = project(total, x_middle, middle)

    own_dest = lax.dynamic_index_in_dim(group_dest, own, 0, keepdims=False)
    own_length = lax.dynamic_index_in_dim(group_length, own, 0, keepdims=False)
    sent = attend(own_dest, own_length, total, x_late, bias, late, packs)
    received = lax.all_to_all(sent, "dp", split_axis=0, concat_axis=0, tiled=True)

    slot = group_offset // GROUP
    hits = (group_dest == own)[None] & (
        slot[None] == jnp.arange(groups, dtype=jnp.int32)[:, None, None]
    )
    packs_of = jnp.arange(packs, dtype=jnp.int32)[None, :, None]
    source = jnp.sum(jnp.where(hits, packs_of, 0), (1, 2)).reshape(planes, -1)
    step = jnp.arange(planes, dtype=jnp.int32)
    source = source[(plane + step) % planes].reshape(-1)
    parts = place(source, received, planes)
    arrived = [parts[0]]
    for k in range(1, planes):
        arrived.append(
            lax.ppermute(parts[k], "mp", [(i, (i + k) % planes) for i in range(planes)])
        )
    return join((plane - step) % planes, arrived)


def solution(mesh):
    return jax.shard_map(
        per_device,
        mesh=mesh,
        in_specs=(
            P("dp", None),
            P(),
            P("dp", "mp"),
            P("dp", "mp"),
            P("mp"),
            P("mp"),
            P(),
            P(),
            P(),
        ),
        out_specs=P(("dp", "mp"), None),
        check_vma=False,
    )
```

```python
import jax
import jax.numpy as jnp
import numpy as np
from jax import lax
from jax.experimental import pallas as pl
from jax.experimental.pallas import tpu as pltpu
from jax.sharding import PartitionSpec as P

HD = 128
GROUP = 64
SIDE = 4
MIB = 1024 * 1024
PIECES = (6, 20, 6)

rope_base = 1000000.0
norm_epsilon = 1e-06


def rope_tables():
    half = HD // 2
    frequency = np.float32(rope_base) ** (
        -(np.arange(half, dtype=np.float32) * np.float32(2.0)) / np.float32(HD)
    )
    within = np.arange(GROUP)
    position = np.concatenate([within % length for length in (64, 32, 16, 8)])
    angles = position.astype(np.float32)[:, None] * frequency[None, :].astype(np.float32)
    cosine, sine = np.cos(angles), np.sin(angles)
    return (
        np.concatenate([cosine, cosine], 1).astype(np.float32),
        np.concatenate([-sine, sine], 1).astype(np.float32),
    )


def device_index(y, z, core):
    return ((y % SIDE) * SIDE + (z % SIDE)) * 2 + core


def shift_pairs(first, second):
    pairs = []
    for y in range(SIDE):
        for z in range(SIDE):
            pairs.append((device_index(y, z, 0), device_index(y + first, z + second, 0)))
            pairs.append((device_index(y, z, 1), device_index(y + second, z + first, 1)))
    return pairs


def swap_pairs():
    return [
        (device_index(y, z, core), device_index(y, z, 1 - core))
        for y in range(SIDE)
        for z in range(SIDE)
        for core in range(2)
    ]


def source_table():
    table = np.zeros((32, 64), np.int32)
    for y in range(SIDE):
        for z in range(SIDE):
            for core in range(2):

                def blocks(c, offsets):
                    found = []
                    for a, b, halves in offsets:
                        held = (
                            device_index(y - a, z - b, c)
                            if c == 0
                            else device_index(y - b, z - a, c)
                        )
                        found += [2 * held + half for half in halves]
                    return found

                both, low, high = (0, 1), (0,), (1,)
                near = [(1, 0, both), (3, 0, both), (2, 0, both)]
                ahead = [(1, 1, both), (3, 1, both), (2, 1, both), (0, 2, low)]
                behind = [(1, 3, both), (3, 3, both), (2, 3, both), (0, 2, high)]
                far = [(1, 2, both), (2, 2, low), (3, 2, both), (2, 2, high)]
                other = 1 - core
                order = blocks(core, [(0, 0, both)] + near + [(0, 1, both), (0, 3, both)])
                order += blocks(other, near + [(0, 1, both), (0, 3, both), (0, 0, both)])
                order += blocks(core, ahead + behind) + blocks(other, ahead + behind)
                order += blocks(core, far) + blocks(other, far)
                table[device_index(y, z, core)] = order
    return table


def norm_kernel(order_ref, hidden_ref, gain_ref, early_ref, middle_ref, late_ref):
    features = hidden_ref.shape[1]
    depth = features // order_ref.shape[0]
    widened = hidden_ref[...].astype(jnp.float32)
    mean_square = jnp.sum(widened * widened, -1, keepdims=True) * (1.0 / features)
    scale = lax.rsqrt(mean_square + norm_epsilon)
    place = 0
    for ref in (early_ref, middle_ref, late_ref):
        for j in range(ref.shape[1] // depth):
            start = pl.multiple_of(order_ref[place] * depth, depth)
            block = hidden_ref[:, pl.ds(start, depth)].astype(jnp.float32)
            gain = gain_ref[:, pl.ds(start, depth)]
            ref[:, j * depth : (j + 1) * depth] = (block * scale * gain).astype(jnp.bfloat16)
            place += 1


def norm(order, hidden, gain, widths):
    rows, features = hidden.shape
    tile = 128
    return pl.pallas_call(
        norm_kernel,
        grid_spec=pltpu.PrefetchScalarGridSpec(
            num_scalar_prefetch=1,
            grid=(rows // tile,),
            in_specs=[
                pl.BlockSpec((tile, features), lambda i, order: (i, 0)),
                pl.BlockSpec((1, features), lambda i, order: (0, 0)),
            ],
            out_specs=[pl.BlockSpec((tile, w), lambda i, order: (i, 0)) for w in widths],
        ),
        out_shape=[jax.ShapeDtypeStruct((rows, w), jnp.bfloat16) for w in widths],
        compiler_params=pltpu.CompilerParams(vmem_limit_bytes=24 * MIB),
        cost_estimate=pl.CostEstimate(
            flops=6 * rows * features, bytes_accessed=4 * rows * features, transcendentals=rows
        ),
        name="norm",
    )(order, hidden, gain)


def product(x_ref, pieces):
    weights = jnp.concatenate([piece[...] for piece in pieces], axis=0)
    return jnp.dot(x_ref[...], weights, preferred_element_type=jnp.float32)


def first_kernel(x_ref, *refs):
    refs[-1][...] = product(x_ref, refs[:-1])


def add_kernel(total_ref, x_ref, *refs):
    refs[-1][...] = total_ref[...] + product(x_ref, refs[:-1])


def whole(shape):
    return pl.BlockSpec(shape, lambda i: (0,) * len(shape), pipeline_mode=pl.Buffered(1))


def matmul_cost(rows, depth, columns, more):
    return pl.CostEstimate(
        flops=2 * rows * depth * columns,
        bytes_accessed=2 * depth * (rows + columns) + 4 * more * rows * columns,
        transcendentals=0,
    )


def project(total, x, pieces):
    rows, depth = x.shape
    columns = pieces[0].shape[1]
    tile = 256
    block = pl.BlockSpec((tile, columns), lambda i: (i, 0))
    x_block = pl.BlockSpec((tile, depth), lambda i: (i, 0))
    weights = [whole(piece.shape) for piece in pieces]
    return pl.pallas_call(
        first_kernel if total is None else add_kernel,
        grid=(rows // tile,),
        in_specs=([] if total is None else [block]) + [x_block] + weights,
        out_specs=block,
        out_shape=jax.ShapeDtypeStruct((rows, columns), jnp.float32),
        input_output_aliases={} if total is None else {0: 0},
        compiler_params=pltpu.CompilerParams(vmem_limit_bytes=44 * MIB),
        cost_estimate=matmul_cost(rows, depth, columns, 1 if total is None else 2),
        name="project",
    )(*([] if total is None else [total]), x, *pieces)


def attend_kernel(
    dest_ref, length_ref, total_ref, x_ref, bias_ref, cosine_ref, sine_ref, *refs
):
    pieces, (out_ref, context, sems) = refs[:-3], refs[-3:]
    step = pl.program_id(0)
    slot = lax.rem(step, 2)
    rows, columns = total_ref.shape
    heads = columns // HD - 2
    groups = rows // GROUP

    def copies(at_step, at_slot):
        return [
            pltpu.make_async_copy(
                context.at[at_slot, pl.ds(g * GROUP, GROUP)],
                out_ref.at[dest_ref[at_step * groups + g]],
                sems.at[at_slot, g],
            )
            for g in range(groups)
        ]

    lengths = [length_ref[step * groups + g] for g in range(groups)]
    row_tables = []
    for table in (cosine_ref, sine_ref):
        parts = []
        for length in lengths:
            index = (
                (length < 64).astype(jnp.int32)
                + (length < 32).astype(jnp.int32)
                + (length < 16).astype(jnp.int32)
            )
            parts.append(table[pl.ds(pl.multiple_of(index * GROUP, GROUP), GROUP), :])
        row_tables.append(jnp.concatenate(parts, 0))
    cosine, sine = row_tables

    summed = total_ref[...] + product(x_ref, pieces) + bias_ref[...]

    def rotated(column):
        head = summed[:, column : column + HD]
        return (head * cosine + pltpu.roll(head, HD // 2, 1) * sine).astype(jnp.bfloat16)

    query = [rotated(h * HD) for h in range(heads)]
    key = rotated(heads * HD)
    value = summed[:, (heads + 1) * HD :].astype(jnp.bfloat16)

    @pl.when(step >= 2)
    def _():
        for copy in copies(step - 2, slot):
            copy.wait()

    tile = 2 * GROUP
    row = lax.broadcasted_iota(jnp.int32, (tile, tile), 0)
    column = lax.broadcasted_iota(jnp.int32, (tile, tile), 1)
    for t in range(rows // tile):
        length = jnp.where(row < GROUP, lengths[2 * t], lengths[2 * t + 1])
        allowed = (column >= (row & -length)) & (column <= row)
        span = slice(t * tile, (t + 1) * tile)
        stacked = jnp.concatenate([q[span] for q in query], 0)
        scores = lax.dot_general(
            stacked, key[span], (((1,), (1,)), ((), ())), preferred_element_type=jnp.float32
        ) * (HD ** (-0.5))
        scores = jnp.where(allowed[None], scores.reshape(heads, tile, tile), -jnp.inf)
        weights = jnp.exp(scores - jnp.max(scores, -1, keepdims=True))
        weights = weights * (1.0 / jnp.sum(weights, -1, keepdims=True))
        weights = weights.astype(jnp.bfloat16).reshape(heads * tile, tile)
        mixed = jnp.dot(weights, value[span], preferred_element_type=jnp.float32)
        mixed = mixed.astype(jnp.bfloat16)
        for h in range(heads):
            context[slot, span, h * HD : (h + 1) * HD] = mixed[h * tile : (h + 1) * tile]

    for copy in copies(step, slot):
        copy.start()

    @pl.when(step == pl.num_programs(0) - 1)
    def _():
        for copy in copies(step - 1, 1 - slot) + copies(step, slot):
            copy.wait()


def attend(dest, lengths, total, x, bias, pieces, packs):
    rows, depth = x.shape
    columns = total.shape[1]
    tile = 256
    cosine, sine = rope_tables()
    width = columns - 2 * HD

    def fixed(shape):
        return pl.BlockSpec(
            shape, lambda i, *_: (0,) * len(shape), pipeline_mode=pl.Buffered(1)
        )

    return pl.pallas_call(
        attend_kernel,
        grid_spec=pltpu.PrefetchScalarGridSpec(
            num_scalar_prefetch=2,
            grid=(rows // tile,),
            in_specs=[
                pl.BlockSpec((tile, columns), lambda i, *_: (i, 0)),
                pl.BlockSpec((tile, depth), lambda i, *_: (i, 0)),
                fixed(bias.shape),
                fixed(cosine.shape),
                fixed(sine.shape),
            ]
            + [fixed(piece.shape) for piece in pieces],
            out_specs=pl.BlockSpec(memory_space=pl.ANY),
            scratch_shapes=[
                pltpu.VMEM((2, tile, width), jnp.bfloat16),
                pltpu.SemaphoreType.DMA((2, tile // GROUP)),
            ],
        ),
        out_shape=jax.ShapeDtypeStruct((packs, GROUP, width), jnp.bfloat16),
        compiler_params=pltpu.CompilerParams(vmem_limit_bytes=48 * MIB),
        cost_estimate=matmul_cost(rows, depth, columns, 2),
        name="attend",
    )(dest, lengths, total, x, bias, cosine, sine, *pieces)


def place_kernel(source_ref, *refs):
    count = len(refs) // 2
    for given, taken in zip(refs[:count], refs[count:], strict=True):
        taken[...] = given[0]


def place(source, received, parts):
    packs, group, width = received.shape
    per_part = source.shape[0] // parts

    def given(part):
        return pl.BlockSpec(
            (1, group, width), lambda j, source: (source[part * per_part + j], 0, 0)
        )

    return pl.pallas_call(
        place_kernel,
        grid_spec=pltpu.PrefetchScalarGridSpec(
            num_scalar_prefetch=1,
            grid=(per_part,),
            in_specs=[given(part) for part in range(parts)],
            out_specs=[pl.BlockSpec((group, width), lambda j, source: (j, 0))] * parts,
        ),
        out_shape=[jax.ShapeDtypeStruct((per_part * group, width), received.dtype)] * parts,
        name="place",
    )(source, *([received] * parts))


def join_kernel(order_ref, *refs):
    width = refs[0].shape[1]
    for part, ref in enumerate(refs[:-1]):
        start = pl.multiple_of(order_ref[part] * width, width)
        refs[-1][:, pl.ds(start, width)] = ref[...]


def join(order, parts):
    rows, width = parts[0].shape
    tile = 64
    return pl.pallas_call(
        join_kernel,
        grid_spec=pltpu.PrefetchScalarGridSpec(
            num_scalar_prefetch=1,
            grid=(rows // tile,),
            in_specs=[pl.BlockSpec((tile, width), lambda i, order: (i, 0))] * len(parts),
            out_specs=pl.BlockSpec((tile, width * len(parts)), lambda i, order: (i, 0)),
        ),
        out_shape=jax.ShapeDtypeStruct((rows, width * len(parts)), parts[0].dtype),
        name="join",
    )(order, *parts)


def per_device(
    hidden_states,
    norm_gain,
    w_query,
    w_keyval,
    query_bias,
    keyval_bias,
    group_dest,
    group_offset,
    group_length,
):
    own = lax.axis_index("dp")
    plane = lax.axis_index("mp")
    planes = lax.axis_size("mp")
    packs, groups = group_dest.shape
    rows, features = hidden_states.shape

    def first(piece, by):
        return lax.ppermute(piece, "dp", shift_pairs(by, 0))

    def second(piece, by):
        return lax.ppermute(piece, "dp", shift_pairs(0, by))

    def swap(piece):
        return lax.ppermute(piece, "dp", swap_pairs())

    weights = jnp.concatenate([w_query, w_keyval], 1)
    bias = jnp.concatenate([query_bias, keyval_bias])[None]
    rows_held = weights.shape[0]
    half = rows_held // 2
    order = lax.dynamic_index_in_dim(jnp.asarray(source_table()), own, 0, keepdims=False)
    near = [first(weights, 1), first(weights, -1), first(weights, 2)]
    own_ahead, own_behind = second(weights, 1), second(weights, -1)
    x_early, x_middle, x_late = norm(
        order, hidden_states, norm_gain[None], [count * rows_held for count in PIECES]
    )

    near, own_ahead, own_behind, x_early = lax.optimization_barrier(
        (near, own_ahead, own_behind, x_early)
    )
    to_ahead = jnp.concatenate([*near, own_ahead[:half]])
    to_behind = jnp.concatenate([*near, own_behind[half:]])
    ahead, behind = second(to_ahead, 1), second(to_behind, -1)
    rest = jnp.concatenate([own_ahead[half:], own_behind, weights])
    middle = [swap(to_ahead), swap(rest)]
    total = project(None, x_early, [weights, *near, own_ahead, own_behind])

    ahead, behind, middle, total = lax.optimization_barrier((ahead, behind, middle, total))
    far = [
        second(jnp.concatenate([ahead[:rows_held], ahead[2 * rows_held : -half * 2]]), 1),
        second(jnp.concatenate([behind[rows_held : 2 * rows_held], behind[-half * 2 : -half]]), -1),
    ]
    middle += [ahead, behind, swap(ahead), swap(behind)]
    total = project(total, x_middle, middle)
    far, total = lax.optimization_barrier((far, total))
    late = far + [swap(piece) for piece in far]

    own_dest = lax.dynamic_index_in_dim(group_dest, own, 0, keepdims=False)
    own_length = lax.dynamic_index_in_dim(group_length, own, 0, keepdims=False)
    sent = attend(own_dest, own_length, total, x_late, bias, late, packs)
    received = lax.all_to_all(sent, "dp", split_axis=0, concat_axis=0, tiled=True)

    slot = group_offset // GROUP
    hits = (group_dest == own)[None] & (
        slot[None] == jnp.arange(groups, dtype=jnp.int32)[:, None, None]
    )
    packs_of = jnp.arange(packs, dtype=jnp.int32)[None, :, None]
    source = jnp.sum(jnp.where(hits, packs_of, 0), (1, 2)).reshape(planes, -1)
    step = jnp.arange(planes, dtype=jnp.int32)
    source = source[(plane + step) % planes].reshape(-1)
    parts = place(source, received, planes)
    arrived = [parts[0]]
    for k in range(1, planes):
        arrived.append(
            lax.ppermute(parts[k], "mp", [(i, (i + k) % planes) for i in range(planes)])
        )
    return join((plane - step) % planes, arrived)


def solution(mesh):
    return jax.shard_map(
        per_device,
        mesh=mesh,
        in_specs=(
            P("dp", None),
            P(),
            P("dp", "mp"),
            P("dp", "mp"),
            P("mp"),
            P("mp"),
            P(),
            P(),
            P(),
        ),
        out_specs=P(("dp", "mp"), None),
        check_vma=False,
    )
```

```python
import functools

import jax
import jax.numpy as jnp
import numpy as np
from jax import lax
from jax.experimental import pallas as pl
from jax.experimental.pallas import tpu as pltpu
from jax.sharding import PartitionSpec as P

HD = 128
GROUP = 64
SIDE = 4
MIB = 1024 * 1024
FIRST_HEADS = 6
PIECES = (12, 12, 4, 4)

rope_base = 1000000.0
norm_epsilon = 1e-06


def rope_tables():
    half = HD // 2
    frequency = np.float32(rope_base) ** (
        -(np.arange(half, dtype=np.float32) * np.float32(2.0)) / np.float32(HD)
    )
    within = np.arange(GROUP)
    position = np.concatenate([within % length for length in (64, 32, 16, 8)])
    angles = position.astype(np.float32)[:, None] * frequency[None, :].astype(np.float32)
    cosine, sine = np.cos(angles), np.sin(angles)
    return (
        np.concatenate([cosine, cosine], 1).astype(np.float32),
        np.concatenate([-sine, sine], 1).astype(np.float32),
    )


def device_index(y, z, core):
    return ((y % SIDE) * SIDE + (z % SIDE)) * 2 + core


def shift_pairs(first, second):
    pairs = []
    for y in range(SIDE):
        for z in range(SIDE):
            pairs.append((device_index(y, z, 0), device_index(y + first, z + second, 0)))
            pairs.append((device_index(y, z, 1), device_index(y + second, z + first, 1)))
    return pairs


def swap_pairs():
    return [
        (device_index(y, z, core), device_index(y, z, 1 - core))
        for y in range(SIDE)
        for z in range(SIDE)
        for core in range(2)
    ]


def source_table():
    table = np.zeros((32, 64), np.int32)
    for y in range(SIDE):
        for z in range(SIDE):
            for core in range(2):

                def blocks(c, offsets):
                    found = []
                    for a, b, halves in offsets:
                        held = (
                            device_index(y - a, z - b, c)
                            if c == 0
                            else device_index(y - b, z - a, c)
                        )
                        found += [2 * held + half for half in halves]
                    return found

                both, low, high = (0, 1), (0,), (1,)
                beside = [(1, 0, both), (3, 0, both), (2, 0, both)]
                straight = [(0, 0, both), (0, 1, both), (0, 3, both)]
                ahead = [(1, 1, both), (3, 1, both), (2, 1, both)]
                behind = [(1, 3, both), (3, 3, both), (2, 3, both)]
                far = [(1, 2, both), (2, 2, low), (0, 2, low)]
                far += [(3, 2, both), (2, 2, high), (0, 2, high)]
                order = []
                for offsets in (beside + straight, ahead + behind, far):
                    order += blocks(core, offsets) + blocks(1 - core, offsets)
                table[device_index(y, z, core)] = order
    return table


def scaled_columns(order_ref, place, hidden_ref, gain_ref, scale, refs):
    depth = hidden_ref.shape[1] // order_ref.shape[0]
    for ref in refs:
        for j in range(ref.shape[1] // depth):
            start = pl.multiple_of(order_ref[place] * depth, depth)
            block = hidden_ref[:, pl.ds(start, depth)].astype(jnp.float32)
            gain = gain_ref[:, pl.ds(start, depth)]
            ref[:, j * depth : (j + 1) * depth] = (block * scale * gain).astype(jnp.bfloat16)
            place += 1


def norm_kernel(order_ref, hidden_ref, gain_ref, scale_ref, *refs):
    widened = hidden_ref[...].astype(jnp.float32)
    mean_square = jnp.sum(widened * widened, -1, keepdims=True) * (1.0 / widened.shape[1])
    scale = lax.rsqrt(mean_square + norm_epsilon)
    scale_ref[...] = scale
    scaled_columns(order_ref, 0, hidden_ref, gain_ref, scale, refs)


def norm_rest_kernel(place, order_ref, hidden_ref, gain_ref, scale_ref, *refs):
    scaled_columns(order_ref, place, hidden_ref, gain_ref, scale_ref[...], refs)


def norm(order, hidden, gain, widths, scale=None, place=0):
    rows, features = hidden.shape
    tile = 128
    given = [hidden, gain] + ([] if scale is None else [scale])
    in_specs = [
        pl.BlockSpec((tile, features), lambda i, order: (i, 0)),
        pl.BlockSpec((1, features), lambda i, order: (0, 0)),
    ]
    out_specs = [pl.BlockSpec((tile, w), lambda i, order: (i, 0)) for w in widths]
    out_shape = [pltpu.HBM((rows, w), jnp.bfloat16) for w in widths]
    scale_spec = pl.BlockSpec((tile, 1), lambda i, order: (i, 0))
    if scale is None:
        out_specs = [scale_spec] + out_specs
        out_shape = [jax.ShapeDtypeStruct((rows, 1), jnp.float32)] + out_shape
    else:
        in_specs = in_specs + [scale_spec]
    return pl.pallas_call(
        norm_kernel if scale is None else functools.partial(norm_rest_kernel, place),
        grid_spec=pltpu.PrefetchScalarGridSpec(
            num_scalar_prefetch=1, grid=(rows // tile,), in_specs=in_specs, out_specs=out_specs
        ),
        out_shape=out_shape,
        compiler_params=pltpu.CompilerParams(vmem_limit_bytes=32 * MIB),
        cost_estimate=pl.CostEstimate(
            flops=6 * rows * features,
            bytes_accessed=2 * rows * (features + sum(widths)),
            transcendentals=rows,
        ),
        name="norm",
    )(order, *given)


def product(x_ref, pieces, columns=slice(None)):
    weights = jnp.concatenate([piece[:, columns] for piece in pieces], axis=0)
    return jnp.dot(x_ref[...], weights, preferred_element_type=jnp.float32)


def tile_rows(tile):
    return pl.ds(pl.multiple_of(pl.program_id(0) * tile, tile), tile)


def first_kernel(x_ref, *refs):
    refs[-1][tile_rows(x_ref.shape[0]), :] = product(x_ref, refs[:-1])


def add_kernel(total_ref, x_ref, *refs):
    rows = tile_rows(x_ref.shape[0])
    refs[-1][rows, :] = total_ref[rows, :] + product(x_ref, refs[:-1])


def matmul_cost(rows, depth, columns, more):
    return pl.CostEstimate(
        flops=2 * rows * depth * columns,
        bytes_accessed=2 * depth * (rows + columns) + 4 * more * rows * columns,
        transcendentals=0,
    )


def project(total, x, pieces):
    rows, depth = x.shape
    columns = pieces[0].shape[1]
    tile = 256
    resident = pl.BlockSpec(memory_space=pltpu.VMEM)
    x_block = pl.BlockSpec((tile, depth), lambda i: (i, 0))
    totals = [] if total is None else [total]
    return pl.pallas_call(
        add_kernel if totals else first_kernel,
        grid=(rows // tile,),
        in_specs=[resident] * len(totals) + [x_block] + [resident] * len(pieces),
        out_specs=resident,
        out_shape=jax.ShapeDtypeStruct((rows, columns), jnp.float32),
        input_output_aliases={0: 0} if totals else {},
        compiler_params=pltpu.CompilerParams(vmem_limit_bytes=20 * MIB),
        cost_estimate=matmul_cost(rows, depth, columns, 2),
        name="project",
    )(*totals, x, *pieces)


def attend_kernel(
    columns, dest_ref, length_ref, total_ref, x_ref, bias_ref, cosine_ref, sine_ref, *refs
):
    makes_keyval = columns.start == 0
    if makes_keyval:
        pieces, (out_ref, keyval_ref, context, sems) = refs[:-4], refs[-4:]
    else:
        keyval_ref, pieces, (out_ref, context, sems) = refs[0], refs[1:-3], refs[-3:]
    step = pl.program_id(0)
    slot = lax.rem(step, 2)
    rows = x_ref.shape[0]
    heads = context.shape[2] // HD
    groups = rows // GROUP

    def copies(at_step, at_slot):
        return [
            pltpu.make_async_copy(
                context.at[at_slot, pl.ds(g * GROUP, GROUP)],
                out_ref.at[dest_ref[at_step * groups + g]],
                sems.at[at_slot, g],
            )
            for g in range(groups)
        ]

    lengths = [length_ref[step * groups + g] for g in range(groups)]
    row_tables = []
    for table in (cosine_ref, sine_ref):
        parts = []
        for length in lengths:
            index = (
                (length < 64).astype(jnp.int32)
                + (length < 32).astype(jnp.int32)
                + (length < 16).astype(jnp.int32)
            )
            parts.append(table[pl.ds(pl.multiple_of(index * GROUP, GROUP), GROUP), :])
        row_tables.append(jnp.concatenate(parts, 0))
    cosine, sine = row_tables

    summed = (
        total_ref[tile_rows(rows), columns]
        + product(x_ref, pieces, columns)
        + bias_ref[:, columns]
    )

    def rotated(column):
        head = summed[:, column : column + HD]
        return (head * cosine + pltpu.roll(head, HD // 2, 1) * sine).astype(jnp.bfloat16)

    query = [rotated(h * HD) for h in range(heads)]
    if makes_keyval:
        key = rotated(heads * HD)
        value = summed[:, (heads + 1) * HD :].astype(jnp.bfloat16)
        keyval_ref[:, :HD] = key
        keyval_ref[:, HD:] = value
    else:
        key, value = keyval_ref[:, :HD], keyval_ref[:, HD:]

    @pl.when(step >= 2)
    def _():
        for copy in copies(step - 2, slot):
            copy.wait()

    tile = 2 * GROUP
    row = lax.broadcasted_iota(jnp.int32, (tile, tile), 0)
    column = lax.broadcasted_iota(jnp.int32, (tile, tile), 1)
    for t in range(rows // tile):
        length = jnp.where(row < GROUP, lengths[2 * t], lengths[2 * t + 1])
        allowed = (column >= (row & -length)) & (column <= row)
        span = slice(t * tile, (t + 1) * tile)
        stacked = jnp.concatenate([q[span] for q in query], 0)
        scores = lax.dot_general(
            stacked, key[span], (((1,), (1,)), ((), ())), preferred_element_type=jnp.float32
        ) * (HD ** (-0.5))
        scores = jnp.where(allowed[None], scores.reshape(heads, tile, tile), -jnp.inf)
        weights = jnp.exp(scores - jnp.max(scores, -1, keepdims=True))
        weights = weights * (1.0 / jnp.sum(weights, -1, keepdims=True))
        weights = weights.astype(jnp.bfloat16).reshape(heads * tile, tile)
        mixed = jnp.dot(weights, value[span], preferred_element_type=jnp.float32)
        mixed = mixed.astype(jnp.bfloat16)
        for h in range(heads):
            context[slot, span, h * HD : (h + 1) * HD] = mixed[h * tile : (h + 1) * tile]

    for copy in copies(step, slot):
        copy.start()

    @pl.when(step == pl.num_programs(0) - 1)
    def _():
        for copy in copies(step - 1, 1 - slot) + copies(step, slot):
            copy.wait()


def attend(dest, lengths, total, x, bias, keyval, pieces, packs, columns):
    rows, depth = x.shape
    tile = 256
    cosine, sine = rope_tables()
    resident = pl.BlockSpec(memory_space=pltpu.VMEM)

    def fixed(shape):
        return pl.BlockSpec(
            shape, lambda i, *_: (0,) * len(shape), pipeline_mode=pl.Buffered(1)
        )

    def by_rows(width):
        return pl.BlockSpec((tile, width), lambda i, *_: (i, 0))

    width = columns.stop - columns.start
    out_specs = [pl.BlockSpec(memory_space=pltpu.HBM)]
    if keyval is None:
        width -= 2 * HD
        out_specs.append(by_rows(2 * HD))
    out_shape = [
        pltpu.HBM((packs, GROUP, width), jnp.bfloat16),
        jax.ShapeDtypeStruct((rows, 2 * HD), jnp.bfloat16),
    ]
    keyvals = [] if keyval is None else [keyval]
    return pl.pallas_call(
        functools.partial(attend_kernel, columns),
        grid_spec=pltpu.PrefetchScalarGridSpec(
            num_scalar_prefetch=2,
            grid=(rows // tile,),
            in_specs=[
                resident,
                by_rows(depth),
                fixed(bias.shape),
                fixed(cosine.shape),
                fixed(sine.shape),
            ]
            + [by_rows(2 * HD)] * len(keyvals)
            + [resident] * len(pieces),
            out_specs=out_specs,
            scratch_shapes=[
                pltpu.VMEM((2, tile, width), jnp.bfloat16),
                pltpu.SemaphoreType.DMA((2, tile // GROUP)),
            ],
        ),
        out_shape=out_shape[: len(out_specs)],
        compiler_params=pltpu.CompilerParams(vmem_limit_bytes=24 * MIB),
        cost_estimate=matmul_cost(rows, depth, columns.stop - columns.start, 2),
        name="attend",
    )(dest, lengths, total, x, bias, cosine, sine, *keyvals, *pieces)


def place_kernel(source_ref, received_ref, *refs):
    parts, sems = refs[:-1], refs[-1]
    per_part = parts[0].shape[0] // GROUP
    copies = [
        pltpu.make_async_copy(
            received_ref.at[source_ref[k * per_part + j]],
            part.at[pl.ds(j * GROUP, GROUP)],
            sems.at[k * per_part + j],
        )
        for k, part in enumerate(parts)
        for j in range(per_part)
    ]
    for copy in copies:
        copy.start()
    for copy in copies:
        copy.wait()


def place(source, received, parts):
    packs, group, width = received.shape
    per_part = source.shape[0] // parts
    return pl.pallas_call(
        place_kernel,
        grid_spec=pltpu.PrefetchScalarGridSpec(
            num_scalar_prefetch=1,
            grid=(1,),
            in_specs=[pl.BlockSpec(memory_space=pltpu.HBM)],
            out_specs=[pl.BlockSpec(memory_space=pltpu.VMEM)] * parts,
            scratch_shapes=[pltpu.SemaphoreType.DMA((source.shape[0],))],
        ),
        out_shape=[jax.ShapeDtypeStruct((per_part * group, width), received.dtype)] * parts,
        compiler_params=pltpu.CompilerParams(vmem_limit_bytes=8 * MIB),
        name="place",
    )(source, received)


def join_kernel(step, start, order_ref, *refs):
    parts, out_ref, sems = refs[:-2], refs[-2], refs[-1]
    if start > 0:
        parts = parts[1:]
    width = parts[0].shape[1]
    copies = []
    for k, part in enumerate(parts):
        column = pl.multiple_of(order_ref[k] * step + start, HD)
        copies.append(
            pltpu.make_async_copy(part, out_ref.at[:, pl.ds(column, width)], sems.at[k])
        )
    for copy in copies:
        copy.start()
    for copy in copies:
        copy.wait()


def join(order, parts, columns, joined=None, start=0):
    rows = parts[0].shape[0]
    whole = pl.BlockSpec(memory_space=pltpu.HBM)
    given = [] if joined is None else [joined]
    return pl.pallas_call(
        functools.partial(join_kernel, columns // len(parts), start),
        grid_spec=pltpu.PrefetchScalarGridSpec(
            num_scalar_prefetch=1,
            grid=(1,),
            in_specs=[whole] * len(given)
            + [pl.BlockSpec(memory_space=pltpu.VMEM)] * len(parts),
            out_specs=whole,
            scratch_shapes=[pltpu.SemaphoreType.DMA((len(parts),))],
        ),
        out_shape=jax.ShapeDtypeStruct((rows, columns), parts[0].dtype),
        input_output_aliases={1: 0} if given else {},
        compiler_params=pltpu.CompilerParams(vmem_limit_bytes=8 * MIB),
        name="join",
    )(order, *given, *parts)


def per_device(
    hidden_states,
    norm_gain,
    w_query,
    w_keyval,
    query_bias,
    keyval_bias,
    group_dest,
    group_offset,
    group_length,
):
    own = lax.axis_index("dp")
    plane = lax.axis_index("mp")
    planes = lax.axis_size("mp")
    packs, groups = group_dest.shape
    rows, features = hidden_states.shape

    def first(piece, by):
        return lax.ppermute(piece, "dp", shift_pairs(by, 0))

    def second(piece, by):
        return lax.ppermute(piece, "dp", shift_pairs(0, by))

    def swap(piece):
        return lax.ppermute(piece, "dp", swap_pairs())

    cut = FIRST_HEADS * HD
    weights = jnp.concatenate([w_query[:, :cut], w_keyval, w_query[:, cut:]], 1)
    bias = jnp.concatenate([query_bias[:cut], keyval_bias, query_bias[cut:]])[None]
    rows_held = weights.shape[0]
    half = rows_held // 2
    order = lax.dynamic_index_in_dim(jnp.asarray(source_table()), own, 0, keepdims=False)
    near = [first(weights, 1), first(weights, -1), first(weights, 2)]
    own_ahead, own_behind = second(weights, 1), second(weights, -1)
    widths = [count * rows_held for count in PIECES]
    gain = norm_gain[None]
    scale, x_early = norm(order, hidden_states, gain, widths[:1])

    near, own_ahead, own_behind, x_early, scale = lax.optimization_barrier(
        (near, own_ahead, own_behind, x_early, scale)
    )
    beside = jnp.concatenate(near)
    straight = jnp.concatenate([weights, own_ahead, own_behind])
    ahead, behind = second(beside, 1), second(beside, -1)
    total = project(None, x_early, [beside, straight, swap(beside), swap(straight)])
    x_middle, x_far, x_last = norm(
        order, hidden_states, gain, widths[1:], scale, widths[0] // half
    )

    ahead, behind, total, x_middle, x_far, x_last = lax.optimization_barrier(
        (ahead, behind, total, x_middle, x_far, x_last)
    )
    far = [
        second(
            jnp.concatenate(
                [ahead[:rows_held], ahead[2 * rows_held : -half], own_ahead[:half]]
            ),
            1,
        ),
        second(
            jnp.concatenate(
                [behind[rows_held : 2 * rows_held], behind[-half:], own_behind[half:]]
            ),
            -1,
        ),
    ]
    total = project(total, x_middle, [ahead, behind, swap(ahead), swap(behind)])
    far, total = lax.optimization_barrier((far, total))
    last = [swap(piece) for piece in far]
    total = project(total, x_far, far)

    own_dest = lax.dynamic_index_in_dim(group_dest, own, 0, keepdims=False)
    own_length = lax.dynamic_index_in_dim(group_length, own, 0, keepdims=False)
    middle = cut + w_keyval.shape[1]
    given = (own_dest, own_length, total, x_last, bias)
    first_sent, keyval = attend(*given, None, last, packs, slice(0, middle))
    (second_sent,) = attend(*given, keyval, last, packs, slice(middle, weights.shape[1]))

    slot = group_offset // GROUP
    hits = (group_dest == own)[None] & (
        slot[None] == jnp.arange(groups, dtype=jnp.int32)[:, None, None]
    )
    packs_of = jnp.arange(packs, dtype=jnp.int32)[None, :, None]
    source = jnp.sum(jnp.where(hits, packs_of, 0), (1, 2)).reshape(planes, -1)
    step = jnp.arange(planes, dtype=jnp.int32)
    source = source[(plane + step) % planes].reshape(-1)
    joins = (plane - step) % planes

    def exchanged(sent):
        received = lax.all_to_all(sent, "dp", split_axis=0, concat_axis=0, tiled=True)
        parts = place(source, received, planes)
        return [parts[0]] + [
            lax.ppermute(parts[k], "mp", [(i, (i + k) % planes) for i in range(planes)])
            for k in range(1, planes)
        ]

    columns = planes * w_query.shape[1]
    joined = join(joins, exchanged(first_sent), columns)
    return join(joins, exchanged(second_sent), columns, joined, cut)


def solution(mesh):
    return jax.shard_map(
        per_device,
        mesh=mesh,
        in_specs=(
            P("dp", None),
            P(),
            P("dp", "mp"),
            P("dp", "mp"),
            P("mp"),
            P("mp"),
            P(),
            P(),
            P(),
        ),
        out_specs=P(("dp", "mp"), None),
        check_vma=False,
    )
```

```python
import functools

import jax
import jax.numpy as jnp
import numpy as np
from jax import lax
from jax.experimental import pallas as pl
from jax.experimental.pallas import tpu as pltpu
from jax.sharding import PartitionSpec as P

HD = 128
GROUP = 64
SIDE = 4
MIB = 1024 * 1024
FIRST_HEADS = 6
PIECES = (6, 12, 6, 4, 4)

rope_base = 1000000.0
norm_epsilon = 1e-06


def rope_tables():
    half = HD // 2
    frequency = np.float32(rope_base) ** (
        -(np.arange(half, dtype=np.float32) * np.float32(2.0)) / np.float32(HD)
    )
    within = np.arange(GROUP)
    position = np.concatenate([within % length for length in (64, 32, 16, 8)])
    angles = position.astype(np.float32)[:, None] * frequency[None, :].astype(np.float32)
    cosine, sine = np.cos(angles), np.sin(angles)
    return (
        np.concatenate([cosine, cosine], 1).astype(np.float32),
        np.concatenate([-sine, sine], 1).astype(np.float32),
    )


def device_index(y, z, core):
    return ((y % SIDE) * SIDE + (z % SIDE)) * 2 + core


def shift_pairs(first, second):
    pairs = []
    for y in range(SIDE):
        for z in range(SIDE):
            pairs.append((device_index(y, z, 0), device_index(y + first, z + second, 0)))
            pairs.append((device_index(y, z, 1), device_index(y + second, z + first, 1)))
    return pairs


def swap_pairs():
    return [
        (device_index(y, z, core), device_index(y, z, 1 - core))
        for y in range(SIDE)
        for z in range(SIDE)
        for core in range(2)
    ]


def source_table():
    table = np.zeros((32, 64), np.int32)
    for y in range(SIDE):
        for z in range(SIDE):
            for core in range(2):

                def blocks(c, offsets):
                    found = []
                    for a, b, halves in offsets:
                        held = (
                            device_index(y - a, z - b, c)
                            if c == 0
                            else device_index(y - b, z - a, c)
                        )
                        found += [2 * held + half for half in halves]
                    return found

                both, low, high = (0, 1), (0,), (1,)
                near = [(1, 0, both), (3, 0, both), (2, 0, both)]
                near += [(0, 0, both), (0, 1, both), (0, 3, both)]
                corners = [(1, 1, both), (3, 1, both), (2, 1, both)]
                corners += [(1, 3, both), (3, 3, both), (2, 3, both)]
                far = [(1, 2, both), (2, 2, low), (0, 2, low)]
                far += [(3, 2, both), (2, 2, high), (0, 2, high)]
                order = []
                for offsets in (near, corners, far):
                    order += blocks(core, offsets) + blocks(1 - core, offsets)
                table[device_index(y, z, core)] = order
    return table


def beside_kernel(query_ref, keyval_ref, out_ref, sems):
    cut = FIRST_HEADS * HD
    middle = cut + keyval_ref.shape[1]
    copies = [
        pltpu.make_async_copy(
            query_ref.at[:, pl.ds(0, cut)], out_ref.at[:, pl.ds(0, cut)], sems.at[0]
        ),
        pltpu.make_async_copy(
            keyval_ref, out_ref.at[:, pl.ds(cut, middle - cut)], sems.at[1]
        ),
        pltpu.make_async_copy(
            query_ref.at[:, pl.ds(cut, query_ref.shape[1] - cut)],
            out_ref.at[:, pl.ds(middle, out_ref.shape[1] - middle)],
            sems.at[2],
        ),
    ]
    for copy in copies:
        copy.start()
    for copy in copies:
        copy.wait()


def side_by_side(w_query, w_keyval):
    rows = w_query.shape[0]
    return pl.pallas_call(
        beside_kernel,
        in_specs=[pl.BlockSpec(memory_space=pltpu.HBM)] * 2,
        out_specs=pl.BlockSpec(memory_space=pltpu.VMEM),
        out_shape=jax.ShapeDtypeStruct(
            (rows, w_query.shape[1] + w_keyval.shape[1]), w_query.dtype
        ),
        scratch_shapes=[pltpu.SemaphoreType.DMA((3,))],
        compiler_params=pltpu.CompilerParams(vmem_limit_bytes=4 * MIB),
        name="side_by_side",
    )(w_query, w_keyval)


def scaled_columns(order_ref, place, hidden_ref, gain_ref, scale, refs):
    depth = hidden_ref.shape[1] // order_ref.shape[0]
    for ref in refs:
        for j in range(ref.shape[1] // depth):
            start = pl.multiple_of(order_ref[place] * depth, depth)
            block = hidden_ref[:, pl.ds(start, depth)].astype(jnp.float32)
            gain = gain_ref[:, pl.ds(start, depth)]
            ref[:, j * depth : (j + 1) * depth] = (block * scale * gain).astype(jnp.bfloat16)
            place += 1


def norm_kernel(order_ref, hidden_ref, gain_ref, scale_ref, *refs):
    widened = hidden_ref[...].astype(jnp.float32)
    mean_square = jnp.sum(widened * widened, -1, keepdims=True) * (1.0 / widened.shape[1])
    scale = lax.rsqrt(mean_square + norm_epsilon)
    scale_ref[...] = scale
    scaled_columns(order_ref, 0, hidden_ref, gain_ref, scale, refs)


def norm_rest_kernel(place, order_ref, hidden_ref, gain_ref, scale_ref, *refs):
    scaled_columns(order_ref, place, hidden_ref, gain_ref, scale_ref[...], refs)


def norm(order, hidden, gain, widths, scale=None, place=0):
    rows, features = hidden.shape
    tile = 128
    given = [hidden, gain] + ([] if scale is None else [scale])
    in_specs = [
        pl.BlockSpec((tile, features), lambda i, order: (i, 0)),
        pl.BlockSpec((1, features), lambda i, order: (0, 0)),
    ]
    out_specs = [pl.BlockSpec((tile, w), lambda i, order: (i, 0)) for w in widths]
    out_shape = [pltpu.HBM((rows, w), jnp.bfloat16) for w in widths]
    scale_spec = pl.BlockSpec((tile, 1), lambda i, order: (i, 0))
    if scale is None:
        out_specs = [scale_spec] + out_specs
        out_shape = [jax.ShapeDtypeStruct((rows, 1), jnp.float32)] + out_shape
    else:
        in_specs = in_specs + [scale_spec]
    return pl.pallas_call(
        norm_kernel if scale is None else functools.partial(norm_rest_kernel, place),
        grid_spec=pltpu.PrefetchScalarGridSpec(
            num_scalar_prefetch=1, grid=(rows // tile,), in_specs=in_specs, out_specs=out_specs
        ),
        out_shape=out_shape,
        compiler_params=pltpu.CompilerParams(vmem_limit_bytes=32 * MIB),
        cost_estimate=pl.CostEstimate(
            flops=6 * rows * features,
            bytes_accessed=2 * rows * (features + sum(widths)),
            transcendentals=rows,
        ),
        name="norm",
    )(order, *given)


def product(x_ref, pieces, columns=slice(None)):
    weights = jnp.concatenate([piece[:, columns] for piece in pieces], axis=0)
    return jnp.dot(x_ref[...], weights, preferred_element_type=jnp.float32)


def tile_rows(tile):
    return pl.ds(pl.multiple_of(pl.program_id(0) * tile, tile), tile)


def first_kernel(x_ref, *refs):
    refs[-1][tile_rows(x_ref.shape[0]), :] = product(x_ref, refs[:-1])


def add_kernel(total_ref, x_ref, *refs):
    rows = tile_rows(x_ref.shape[0])
    refs[-1][rows, :] = total_ref[rows, :] + product(x_ref, refs[:-1])


def matmul_cost(rows, depth, columns, more):
    return pl.CostEstimate(
        flops=2 * rows * depth * columns,
        bytes_accessed=2 * depth * (rows + columns) + 4 * more * rows * columns,
        transcendentals=0,
    )


def project(total, x, pieces):
    rows, depth = x.shape
    columns = pieces[0].shape[1]
    tile = 256
    resident = pl.BlockSpec(memory_space=pltpu.VMEM)
    x_block = pl.BlockSpec((tile, depth), lambda i: (i, 0))
    totals = [] if total is None else [total]
    return pl.pallas_call(
        add_kernel if totals else first_kernel,
        grid=(rows // tile,),
        in_specs=[resident] * len(totals) + [x_block] + [resident] * len(pieces),
        out_specs=resident,
        out_shape=jax.ShapeDtypeStruct((rows, columns), jnp.float32),
        input_output_aliases={0: 0} if totals else {},
        compiler_params=pltpu.CompilerParams(vmem_limit_bytes=20 * MIB),
        cost_estimate=matmul_cost(rows, depth, columns, 2),
        name="project",
    )(*totals, x, *pieces)


def attend_kernel(
    columns, dest_ref, length_ref, total_ref, x_ref, bias_ref, cosine_ref, sine_ref, *refs
):
    makes_keyval = columns.start == 0
    if makes_keyval:
        pieces, (out_ref, keyval_ref, context, sems) = refs[:-4], refs[-4:]
    else:
        keyval_ref, pieces, (out_ref, context, sems) = refs[0], refs[1:-3], refs[-3:]
    step = pl.program_id(0)
    slot = lax.rem(step, 2)
    rows = x_ref.shape[0]
    heads = context.shape[2] // HD
    groups = rows // GROUP

    def copies(at_step, at_slot):
        return [
            pltpu.make_async_copy(
                context.at[at_slot, pl.ds(g * GROUP, GROUP)],
                out_ref.at[dest_ref[at_step * groups + g]],
                sems.at[at_slot, g],
            )
            for g in range(groups)
        ]

    lengths = [length_ref[step * groups + g] for g in range(groups)]
    row_tables = []
    for table in (cosine_ref, sine_ref):
        parts = []
        for length in lengths:
            index = (
                (length < 64).astype(jnp.int32)
                + (length < 32).astype(jnp.int32)
                + (length < 16).astype(jnp.int32)
            )
            parts.append(table[pl.ds(pl.multiple_of(index * GROUP, GROUP), GROUP), :])
        row_tables.append(jnp.concatenate(parts, 0))
    cosine, sine = row_tables

    summed = (
        total_ref[tile_rows(rows), columns]
        + product(x_ref, pieces, columns)
        + bias_ref[:, columns]
    )

    def rotated(column):
        head = summed[:, column : column + HD]
        return (head * cosine + pltpu.roll(head, HD // 2, 1) * sine).astype(jnp.bfloat16)

    query = [rotated(h * HD) for h in range(heads)]
    if makes_keyval:
        key = rotated(heads * HD)
        value = summed[:, (heads + 1) * HD :].astype(jnp.bfloat16)
        keyval_ref[:, :HD] = key
        keyval_ref[:, HD:] = value
    else:
        key, value = keyval_ref[:, :HD], keyval_ref[:, HD:]

    @pl.when(step >= 2)
    def _():
        for copy in copies(step - 2, slot):
            copy.wait()

    tile = 2 * GROUP
    row = lax.broadcasted_iota(jnp.int32, (tile, tile), 0)
    column = lax.broadcasted_iota(jnp.int32, (tile, tile), 1)
    for t in range(rows // tile):
        length = jnp.where(row < GROUP, lengths[2 * t], lengths[2 * t + 1])
        allowed = (column >= (row & -length)) & (column <= row)
        span = slice(t * tile, (t + 1) * tile)
        stacked = jnp.concatenate([q[span] for q in query], 0)
        scores = lax.dot_general(
            stacked, key[span], (((1,), (1,)), ((), ())), preferred_element_type=jnp.float32
        ) * (HD ** (-0.5))
        scores = jnp.where(allowed[None], scores.reshape(heads, tile, tile), -jnp.inf)
        weights = jnp.exp(scores - jnp.max(scores, -1, keepdims=True))
        weights = weights * (1.0 / jnp.sum(weights, -1, keepdims=True))
        weights = weights.astype(jnp.bfloat16).reshape(heads * tile, tile)
        mixed = jnp.dot(weights, value[span], preferred_element_type=jnp.float32)
        mixed = mixed.astype(jnp.bfloat16)
        for h in range(heads):
            context[slot, span, h * HD : (h + 1) * HD] = mixed[h * tile : (h + 1) * tile]

    for copy in copies(step, slot):
        copy.start()

    @pl.when(step == pl.num_programs(0) - 1)
    def _():
        for copy in copies(step - 1, 1 - slot) + copies(step, slot):
            copy.wait()


def attend(dest, lengths, total, x, bias, keyval, pieces, packs, columns):
    rows, depth = x.shape
    tile = 256
    cosine, sine = rope_tables()
    resident = pl.BlockSpec(memory_space=pltpu.VMEM)

    def fixed(shape):
        return pl.BlockSpec(
            shape, lambda i, *_: (0,) * len(shape), pipeline_mode=pl.Buffered(1)
        )

    def by_rows(width):
        return pl.BlockSpec((tile, width), lambda i, *_: (i, 0))

    width = columns.stop - columns.start
    out_specs = [pl.BlockSpec(memory_space=pltpu.HBM)]
    if keyval is None:
        width -= 2 * HD
        out_specs.append(by_rows(2 * HD))
    out_shape = [
        pltpu.HBM((packs, GROUP, width), jnp.bfloat16),
        jax.ShapeDtypeStruct((rows, 2 * HD), jnp.bfloat16),
    ]
    keyvals = [] if keyval is None else [keyval]
    return pl.pallas_call(
        functools.partial(attend_kernel, columns),
        grid_spec=pltpu.PrefetchScalarGridSpec(
            num_scalar_prefetch=2,
            grid=(rows // tile,),
            in_specs=[
                resident,
                by_rows(depth),
                fixed(bias.shape),
                fixed(cosine.shape),
                fixed(sine.shape),
            ]
            + [by_rows(2 * HD)] * len(keyvals)
            + [resident] * len(pieces),
            out_specs=out_specs,
            scratch_shapes=[
                pltpu.VMEM((2, tile, width), jnp.bfloat16),
                pltpu.SemaphoreType.DMA((2, tile // GROUP)),
            ],
        ),
        out_shape=out_shape[: len(out_specs)],
        compiler_params=pltpu.CompilerParams(vmem_limit_bytes=24 * MIB),
        cost_estimate=matmul_cost(rows, depth, columns.stop - columns.start, 2),
        name="attend",
    )(dest, lengths, total, x, bias, cosine, sine, *keyvals, *pieces)


def place_kernel(source_ref, received_ref, *parts):
    per_part = parts[0].shape[0] // GROUP
    for k, part in enumerate(parts):
        for j in range(per_part):
            part[j * GROUP : (j + 1) * GROUP, :] = received_ref[source_ref[k * per_part + j]]


def place(source, received, parts):
    packs, group, width = received.shape
    per_part = source.shape[0] // parts
    resident = pl.BlockSpec(memory_space=pltpu.VMEM)
    return pl.pallas_call(
        place_kernel,
        grid_spec=pltpu.PrefetchScalarGridSpec(
            num_scalar_prefetch=1,
            grid=(1,),
            in_specs=[resident],
            out_specs=[resident] * parts,
        ),
        out_shape=[jax.ShapeDtypeStruct((per_part * group, width), received.dtype)] * parts,
        compiler_params=pltpu.CompilerParams(vmem_limit_bytes=8 * MIB),
        name="place",
    )(source, received)


def join_kernel(step, start, order_ref, *refs):
    parts, out_ref, sems = refs[:-2], refs[-2], refs[-1]
    if start > 0:
        parts = parts[1:]
    width = parts[0].shape[1]
    copies = []
    for k, part in enumerate(parts):
        column = pl.multiple_of(order_ref[k] * step + start, HD)
        copies.append(
            pltpu.make_async_copy(part, out_ref.at[:, pl.ds(column, width)], sems.at[k])
        )
    for copy in copies:
        copy.start()
    for copy in copies:
        copy.wait()


def join(order, parts, columns, joined=None, start=0):
    rows = parts[0].shape[0]
    whole = pl.BlockSpec(memory_space=pltpu.HBM)
    given = [] if joined is None else [joined]
    return pl.pallas_call(
        functools.partial(join_kernel, columns // len(parts), start),
        grid_spec=pltpu.PrefetchScalarGridSpec(
            num_scalar_prefetch=1,
            grid=(1,),
            in_specs=[whole] * len(given)
            + [pl.BlockSpec(memory_space=pltpu.VMEM)] * len(parts),
            out_specs=whole,
            scratch_shapes=[pltpu.SemaphoreType.DMA((len(parts),))],
        ),
        out_shape=jax.ShapeDtypeStruct((rows, columns), parts[0].dtype),
        input_output_aliases={1: 0} if given else {},
        compiler_params=pltpu.CompilerParams(vmem_limit_bytes=8 * MIB),
        name="join",
    )(order, *given, *parts)


def held_until(value, *others):
    return lax.optimization_barrier((value, *others))[0]


def per_device(
    hidden_states,
    norm_gain,
    w_query,
    w_keyval,
    query_bias,
    keyval_bias,
    group_dest,
    group_offset,
    group_length,
):
    own = lax.axis_index("dp")
    plane = lax.axis_index("mp")
    planes = lax.axis_size("mp")
    packs, groups = group_dest.shape
    rows, features = hidden_states.shape

    def first(piece, by):
        return lax.ppermute(piece, "dp", shift_pairs(by, 0))

    def second(piece, by):
        return lax.ppermute(piece, "dp", shift_pairs(0, by))

    def swap(piece):
        return lax.ppermute(piece, "dp", swap_pairs())

    own_dest = lax.dynamic_index_in_dim(group_dest, own, 0, keepdims=False)
    own_length = lax.dynamic_index_in_dim(group_length, own, 0, keepdims=False)
    slot = group_offset // GROUP
    hits = (group_dest == own)[None] & (
        slot[None] == jnp.arange(groups, dtype=jnp.int32)[:, None, None]
    )
    packs_of = jnp.arange(packs, dtype=jnp.int32)[None, :, None]
    source = jnp.sum(jnp.where(hits, packs_of, 0), (1, 2)).reshape(planes, -1)
    step = jnp.arange(planes, dtype=jnp.int32)
    source = source[(plane + step) % planes].reshape(-1)
    joins = (plane - step) % planes
    plan = own_dest, own_length, source, joins

    cut = FIRST_HEADS * HD
    weights = side_by_side(w_query, w_keyval)
    bias = jnp.concatenate([query_bias[:cut], keyval_bias, query_bias[cut:]])[None]
    rows_held = weights.shape[0]
    half = rows_held // 2
    order = lax.dynamic_index_in_dim(jnp.asarray(source_table()), own, 0, keepdims=False)
    widths = [count * rows_held for count in PIECES]
    gain = norm_gain[None]

    near = [first(weights, 1), first(weights, -1), first(weights, 2)]
    near += [second(weights, 1), second(weights, -1)]
    scale, x_near = norm(order, hidden_states, gain, widths[:1])
    near, scale, x_near, plan, bias = lax.optimization_barrier((near, scale, x_near, plan, bias))
    own_dest, own_length, source, joins = plan

    own_ahead, own_behind = near[3:]
    beside = jnp.concatenate(near[:3])
    ahead, behind = second(beside, 1), second(beside, -1)
    x_middle, x_corners, x_far, x_last = norm(
        order, hidden_states, gain, widths[1:], scale, widths[0] // half
    )
    straight = jnp.concatenate([weights, own_ahead, own_behind])
    total = project(None, x_near, [beside, straight])

    ahead, behind, total, x_middle, x_corners, x_far, x_last = lax.optimization_barrier(
        (ahead, behind, total, x_middle, x_corners, x_far, x_last)
    )
    far = [
        second(
            jnp.concatenate(
                [ahead[:rows_held], ahead[2 * rows_held : -half], own_ahead[:half]]
            ),
            1,
        ),
        second(
            jnp.concatenate(
                [behind[rows_held : 2 * rows_held], behind[-half:], own_behind[half:]]
            ),
            -1,
        ),
    ]
    near = [swap(held_until(piece, ahead)) for piece in (beside, straight)]
    total = project(total, x_middle, [*near, ahead, behind])
    total = project(total, x_corners, [swap(ahead), swap(behind)])
    far, total = lax.optimization_barrier((far, total))
    last = [swap(piece) for piece in far]
    total = project(total, x_far, far)

    middle = cut + w_keyval.shape[1]
    given = (own_dest, own_length, total, x_last, bias)
    first_sent, keyval = attend(*given, None, last, packs, slice(0, middle))
    (second_sent,) = attend(*given, keyval, last, packs, slice(middle, weights.shape[1]))

    def exchanged(sent):
        received = lax.all_to_all(sent, "dp", split_axis=0, concat_axis=0, tiled=True)
        parts = place(source, received, planes)
        return [parts[0]] + [
            lax.ppermute(parts[k], "mp", [(i, (i + k) % planes) for i in range(planes)])
            for k in range(1, planes)
        ]

    columns = planes * w_query.shape[1]
    joined = join(joins, exchanged(first_sent), columns)
    return join(joins, exchanged(second_sent), columns, joined, cut)


def solution(mesh):
    return jax.shard_map(
        per_device,
        mesh=mesh,
        in_specs=(
            P("dp", None),
            P(),
            P("dp", "mp"),
            P("dp", "mp"),
            P("mp"),
            P("mp"),
            P(),
            P(),
            P(),
        ),
        out_specs=P(("dp", "mp"), None),
        check_vma=False,
    )
```

```python
import functools

import jax
import jax.numpy as jnp
import numpy as np
from jax import lax
from jax.experimental import pallas as pl
from jax.experimental.pallas import tpu as pltpu
from jax.sharding import PartitionSpec as P

HD = 128
GROUP = 64
SIDE = 4
MIB = 1024 * 1024
FIRST_HEADS = 6
PIECES = (6, 12, 6, 4, 4)

rope_base = 1000000.0
norm_epsilon = 1e-06


def rope_tables():
    half = HD // 2
    frequency = np.float32(rope_base) ** (
        -(np.arange(half, dtype=np.float32) * np.float32(2.0)) / np.float32(HD)
    )
    within = np.arange(GROUP)
    position = np.concatenate([within % length for length in (64, 32, 16, 8)])
    angles = position.astype(np.float32)[:, None] * frequency[None, :].astype(np.float32)
    cosine, sine = np.cos(angles), np.sin(angles)
    return (
        np.concatenate([cosine, cosine], 1).astype(np.float32),
        np.concatenate([-sine, sine], 1).astype(np.float32),
    )


def device_index(y, z, core):
    return ((y % SIDE) * SIDE + (z % SIDE)) * 2 + core


def shift_pairs(first, second):
    pairs = []
    for y in range(SIDE):
        for z in range(SIDE):
            pairs.append((device_index(y, z, 0), device_index(y + first, z + second, 0)))
            pairs.append((device_index(y, z, 1), device_index(y + second, z + first, 1)))
    return pairs


def swap_pairs():
    return [
        (device_index(y, z, core), device_index(y, z, 1 - core))
        for y in range(SIDE)
        for z in range(SIDE)
        for core in range(2)
    ]


def source_table():
    table = np.zeros((32, 64), np.int32)
    for y in range(SIDE):
        for z in range(SIDE):
            for core in range(2):

                def blocks(c, offsets):
                    found = []
                    for a, b, halves in offsets:
                        held = (
                            device_index(y - a, z - b, c)
                            if c == 0
                            else device_index(y - b, z - a, c)
                        )
                        found += [2 * held + half for half in halves]
                    return found

                both, low, high = (0, 1), (0,), (1,)
                near = [(1, 0, both), (3, 0, both), (2, 0, both)]
                near += [(0, 0, both), (0, 1, both), (0, 3, both)]
                corners = [(1, 1, both), (3, 1, both), (2, 1, both)]
                corners += [(1, 3, both), (3, 3, both), (2, 3, both)]
                far = [(1, 2, both), (2, 2, low), (0, 2, low)]
                far += [(3, 2, both), (2, 2, high), (0, 2, high)]
                order = []
                for offsets in (near, corners, far):
                    order += blocks(core, offsets) + blocks(1 - core, offsets)
                table[device_index(y, z, core)] = order
    return table


def beside_kernel(query_ref, keyval_ref, out_ref, sems):
    cut = FIRST_HEADS * HD
    middle = cut + keyval_ref.shape[1]
    copies = [
        pltpu.make_async_copy(
            query_ref.at[:, pl.ds(0, cut)], out_ref.at[:, pl.ds(0, cut)], sems.at[0]
        ),
        pltpu.make_async_copy(
            keyval_ref, out_ref.at[:, pl.ds(cut, middle - cut)], sems.at[1]
        ),
        pltpu.make_async_copy(
            query_ref.at[:, pl.ds(cut, query_ref.shape[1] - cut)],
            out_ref.at[:, pl.ds(middle, out_ref.shape[1] - middle)],
            sems.at[2],
        ),
    ]
    for copy in copies:
        copy.start()
    for copy in copies:
        copy.wait()


def side_by_side(w_query, w_keyval):
    rows = w_query.shape[0]
    return pl.pallas_call(
        beside_kernel,
        in_specs=[pl.BlockSpec(memory_space=pltpu.HBM)] * 2,
        out_specs=pl.BlockSpec(memory_space=pltpu.VMEM),
        out_shape=jax.ShapeDtypeStruct(
            (rows, w_query.shape[1] + w_keyval.shape[1]), w_query.dtype
        ),
        scratch_shapes=[pltpu.SemaphoreType.DMA((3,))],
        compiler_params=pltpu.CompilerParams(vmem_limit_bytes=58 * MIB),
        name="side_by_side",
    )(w_query, w_keyval)


def scaled_columns(order_ref, place, hidden_ref, gain_ref, scale, refs):
    depth = hidden_ref.shape[1] // order_ref.shape[0]
    for ref in refs:
        for j in range(ref.shape[1] // depth):
            start = pl.multiple_of(order_ref[place] * depth, depth)
            block = hidden_ref[:, pl.ds(start, depth)].astype(jnp.float32)
            gain = gain_ref[:, pl.ds(start, depth)]
            ref[:, j * depth : (j + 1) * depth] = (block * scale * gain).astype(jnp.bfloat16)
            place += 1


def norm_kernel(order_ref, hidden_ref, gain_ref, scale_ref, *refs):
    widened = hidden_ref[...].astype(jnp.float32)
    mean_square = jnp.sum(widened * widened, -1, keepdims=True) * (1.0 / widened.shape[1])
    scale = lax.rsqrt(mean_square + norm_epsilon)
    scale_ref[...] = scale
    scaled_columns(order_ref, 0, hidden_ref, gain_ref, scale, refs)


def norm_rest_kernel(place, order_ref, hidden_ref, gain_ref, scale_ref, *refs):
    scaled_columns(order_ref, place, hidden_ref, gain_ref, scale_ref[...], refs)


def norm(order, hidden, gain, widths, scale=None, place=0):
    rows, features = hidden.shape
    tile = 128
    given = [hidden, gain] + ([] if scale is None else [scale])
    in_specs = [
        pl.BlockSpec((tile, features), lambda i, order: (i, 0)),
        pl.BlockSpec((1, features), lambda i, order: (0, 0)),
    ]
    out_specs = [pl.BlockSpec((tile, w), lambda i, order: (i, 0)) for w in widths]
    out_shape = [pltpu.HBM((rows, w), jnp.bfloat16) for w in widths]
    scale_spec = pl.BlockSpec((tile, 1), lambda i, order: (i, 0))
    if scale is None:
        out_specs = [scale_spec] + out_specs
        out_shape = [jax.ShapeDtypeStruct((rows, 1), jnp.float32)] + out_shape
    else:
        in_specs = in_specs + [scale_spec]
    return pl.pallas_call(
        norm_kernel if scale is None else functools.partial(norm_rest_kernel, place),
        grid_spec=pltpu.PrefetchScalarGridSpec(
            num_scalar_prefetch=1, grid=(rows // tile,), in_specs=in_specs, out_specs=out_specs
        ),
        out_shape=out_shape,
        compiler_params=pltpu.CompilerParams(vmem_limit_bytes=18 * MIB),
        cost_estimate=pl.CostEstimate(
            flops=6 * rows * features,
            bytes_accessed=2 * rows * (features + sum(widths)),
            transcendentals=rows,
        ),
        name="norm",
    )(order, *given)


def product(x_ref, pieces, columns=slice(None)):
    weights = jnp.concatenate([piece[:, columns] for piece in pieces], axis=0)
    return jnp.dot(x_ref[...], weights, preferred_element_type=jnp.float32)


def tile_rows(tile):
    return pl.ds(pl.multiple_of(pl.program_id(0) * tile, tile), tile)


def first_kernel(x_ref, *refs):
    refs[-1][tile_rows(x_ref.shape[0]), :] = product(x_ref, refs[:-1])


def add_kernel(total_ref, x_ref, *refs):
    rows = tile_rows(x_ref.shape[0])
    refs[-1][rows, :] = total_ref[rows, :] + product(x_ref, refs[:-1])


def matmul_cost(rows, depth, columns, more):
    return pl.CostEstimate(
        flops=2 * rows * depth * columns,
        bytes_accessed=2 * depth * (rows + columns) + 4 * more * rows * columns,
        transcendentals=0,
    )


def project(total, x, pieces):
    rows, depth = x.shape
    columns = pieces[0].shape[1]
    tile = 256
    resident = pl.BlockSpec(memory_space=pltpu.VMEM)
    x_block = pl.BlockSpec((tile, depth), lambda i: (i, 0))
    totals = [] if total is None else [total]
    return pl.pallas_call(
        add_kernel if totals else first_kernel,
        grid=(rows // tile,),
        in_specs=[resident] * len(totals) + [x_block] + [resident] * len(pieces),
        out_specs=resident,
        out_shape=jax.ShapeDtypeStruct((rows, columns), jnp.float32),
        input_output_aliases={0: 0} if totals else {},
        compiler_params=pltpu.CompilerParams(vmem_limit_bytes=20 * MIB),
        cost_estimate=matmul_cost(rows, depth, columns, 2),
        name="project",
    )(*totals, x, *pieces)


def attend_kernel(
    columns, dest_ref, length_ref, total_ref, x_ref, bias_ref, cosine_ref, sine_ref, *refs
):
    makes_keyval = columns.start == 0
    if makes_keyval:
        pieces, (out_ref, keyval_ref, context, sems) = refs[:-4], refs[-4:]
    else:
        keyval_ref, pieces, (out_ref, context, sems) = refs[0], refs[1:-3], refs[-3:]
    step = pl.program_id(0)
    slot = lax.rem(step, 2)
    rows = x_ref.shape[0]
    heads = context.shape[2] // HD
    groups = rows // GROUP

    def copies(at_step, at_slot):
        return [
            pltpu.make_async_copy(
                context.at[at_slot, pl.ds(g * GROUP, GROUP)],
                out_ref.at[dest_ref[at_step * groups + g]],
                sems.at[at_slot, g],
            )
            for g in range(groups)
        ]

    lengths = [length_ref[step * groups + g] for g in range(groups)]
    row_tables = []
    for table in (cosine_ref, sine_ref):
        parts = []
        for length in lengths:
            index = (
                (length < 64).astype(jnp.int32)
                + (length < 32).astype(jnp.int32)
                + (length < 16).astype(jnp.int32)
            )
            parts.append(table[pl.ds(pl.multiple_of(index * GROUP, GROUP), GROUP), :])
        row_tables.append(jnp.concatenate(parts, 0))
    cosine, sine = row_tables

    summed = (
        total_ref[tile_rows(rows), columns]
        + product(x_ref, pieces, columns)
        + bias_ref[:, columns]
    )

    def rotated(column):
        head = summed[:, column : column + HD]
        return (head * cosine + pltpu.roll(head, HD // 2, 1) * sine).astype(jnp.bfloat16)

    query = [rotated(h * HD) for h in range(heads)]
    if makes_keyval:
        key = rotated(heads * HD)
        value = summed[:, (heads + 1) * HD :].astype(jnp.bfloat16)
        keyval_ref[:, :HD] = key
        keyval_ref[:, HD:] = value
    else:
        key, value = keyval_ref[:, :HD], keyval_ref[:, HD:]

    @pl.when(step >= 2)
    def _():
        for copy in copies(step - 2, slot):
            copy.wait()

    tile = 2 * GROUP
    row = lax.broadcasted_iota(jnp.int32, (tile, tile), 0)
    column = lax.broadcasted_iota(jnp.int32, (tile, tile), 1)
    for t in range(rows // tile):
        length = jnp.where(row < GROUP, lengths[2 * t], lengths[2 * t + 1])
        allowed = (column >= (row & -length)) & (column <= row)
        span = slice(t * tile, (t + 1) * tile)
        stacked = jnp.concatenate([q[span] for q in query], 0)
        scores = lax.dot_general(
            stacked, key[span], (((1,), (1,)), ((), ())), preferred_element_type=jnp.float32
        ) * (HD ** (-0.5))
        scores = jnp.where(allowed[None], scores.reshape(heads, tile, tile), -jnp.inf)
        weights = jnp.exp(scores - jnp.max(scores, -1, keepdims=True))
        weights = weights * (1.0 / jnp.sum(weights, -1, keepdims=True))
        weights = weights.astype(jnp.bfloat16).reshape(heads * tile, tile)
        mixed = jnp.dot(weights, value[span], preferred_element_type=jnp.float32)
        mixed = mixed.astype(jnp.bfloat16)
        for h in range(heads):
            context[slot, span, h * HD : (h + 1) * HD] = mixed[h * tile : (h + 1) * tile]

    for copy in copies(step, slot):
        copy.start()

    @pl.when(step == pl.num_programs(0) - 1)
    def _():
        for copy in copies(step - 1, 1 - slot) + copies(step, slot):
            copy.wait()


def attend(dest, lengths, total, x, bias, keyval, pieces, packs, columns):
    rows, depth = x.shape
    tile = 512
    cosine, sine = rope_tables()
    resident = pl.BlockSpec(memory_space=pltpu.VMEM)

    def fixed(shape):
        return pl.BlockSpec(
            shape, lambda i, *_: (0,) * len(shape), pipeline_mode=pl.Buffered(1)
        )

    def by_rows(width):
        return pl.BlockSpec((tile, width), lambda i, *_: (i, 0))

    width = columns.stop - columns.start
    out_specs = [pl.BlockSpec(memory_space=pltpu.HBM)]
    if keyval is None:
        width -= 2 * HD
        out_specs.append(by_rows(2 * HD))
    out_shape = [
        pltpu.HBM((packs, GROUP, width), jnp.bfloat16),
        jax.ShapeDtypeStruct((rows, 2 * HD), jnp.bfloat16),
    ]
    keyvals = [] if keyval is None else [keyval]
    return pl.pallas_call(
        functools.partial(attend_kernel, columns),
        grid_spec=pltpu.PrefetchScalarGridSpec(
            num_scalar_prefetch=2,
            grid=(rows // tile,),
            in_specs=[
                resident,
                by_rows(depth),
                fixed(bias.shape),
                fixed(cosine.shape),
                fixed(sine.shape),
            ]
            + [by_rows(2 * HD)] * len(keyvals)
            + [resident] * len(pieces),
            out_specs=out_specs,
            scratch_shapes=[
                pltpu.VMEM((2, tile, width), jnp.bfloat16),
                pltpu.SemaphoreType.DMA((2, tile // GROUP)),
            ],
        ),
        out_shape=out_shape[: len(out_specs)],
        compiler_params=pltpu.CompilerParams(vmem_limit_bytes=28 * MIB),
        cost_estimate=matmul_cost(rows, depth, columns.stop - columns.start, 2),
        name="attend",
    )(dest, lengths, total, x, bias, cosine, sine, *keyvals, *pieces)


def place_kernel(source_ref, received_ref, *parts):
    per_part = parts[0].shape[0] // GROUP
    for k, part in enumerate(parts):
        for j in range(per_part):
            part[j * GROUP : (j + 1) * GROUP, :] = received_ref[source_ref[k * per_part + j]]


def place(source, received, parts):
    packs, group, width = received.shape
    per_part = source.shape[0] // parts
    resident = pl.BlockSpec(memory_space=pltpu.VMEM)
    return pl.pallas_call(
        place_kernel,
        grid_spec=pltpu.PrefetchScalarGridSpec(
            num_scalar_prefetch=1,
            grid=(1,),
            in_specs=[resident],
            out_specs=[resident] * parts,
        ),
        out_shape=[jax.ShapeDtypeStruct((per_part * group, width), received.dtype)] * parts,
        compiler_params=pltpu.CompilerParams(vmem_limit_bytes=8 * MIB),
        name="place",
    )(source, received)


def join_kernel(step, start, order_ref, *refs):
    parts, out_ref, sems = refs[:-2], refs[-2], refs[-1]
    if start > 0:
        parts = parts[1:]
    width = parts[0].shape[1]
    copies = []
    for k, part in enumerate(parts):
        column = pl.multiple_of(order_ref[k] * step + start, HD)
        copies.append(
            pltpu.make_async_copy(part, out_ref.at[:, pl.ds(column, width)], sems.at[k])
        )
    for copy in copies:
        copy.start()
    for copy in copies:
        copy.wait()


def join(order, parts, columns, joined=None, start=0):
    rows = parts[0].shape[0]
    whole = pl.BlockSpec(memory_space=pltpu.HBM)
    given = [] if joined is None else [joined]
    return pl.pallas_call(
        functools.partial(join_kernel, columns // len(parts), start),
        grid_spec=pltpu.PrefetchScalarGridSpec(
            num_scalar_prefetch=1,
            grid=(1,),
            in_specs=[whole] * len(given)
            + [pl.BlockSpec(memory_space=pltpu.VMEM)] * len(parts),
            out_specs=whole,
            scratch_shapes=[pltpu.SemaphoreType.DMA((len(parts),))],
        ),
        out_shape=jax.ShapeDtypeStruct((rows, columns), parts[0].dtype),
        input_output_aliases={1: 0} if given else {},
        compiler_params=pltpu.CompilerParams(vmem_limit_bytes=8 * MIB),
        name="join",
    )(order, *given, *parts)


def held_until(value, *others):
    return lax.optimization_barrier((value, *others))[0]


def per_device(
    hidden_states,
    norm_gain,
    w_query,
    w_keyval,
    query_bias,
    keyval_bias,
    group_dest,
    group_offset,
    group_length,
):
    own = lax.axis_index("dp")
    plane = lax.axis_index("mp")
    planes = lax.axis_size("mp")
    packs, groups = group_dest.shape
    rows, features = hidden_states.shape

    def first(piece, by):
        return lax.ppermute(piece, "dp", shift_pairs(by, 0))

    def second(piece, by):
        return lax.ppermute(piece, "dp", shift_pairs(0, by))

    def swap(piece):
        return lax.ppermute(piece, "dp", swap_pairs())

    own_dest = lax.dynamic_index_in_dim(group_dest, own, 0, keepdims=False)
    own_length = lax.dynamic_index_in_dim(group_length, own, 0, keepdims=False)
    slot = group_offset // GROUP
    hits = (group_dest == own)[None] & (
        slot[None] == jnp.arange(groups, dtype=jnp.int32)[:, None, None]
    )
    packs_of = jnp.arange(packs, dtype=jnp.int32)[None, :, None]
    source = jnp.sum(jnp.where(hits, packs_of, 0), (1, 2)).reshape(planes, -1)
    step = jnp.arange(planes, dtype=jnp.int32)
    source = source[(plane + step) % planes].reshape(-1)
    joins = (plane - step) % planes
    plan = own_dest, own_length, source, joins

    cut = FIRST_HEADS * HD
    weights = side_by_side(w_query, w_keyval)
    bias = jnp.concatenate([query_bias[:cut], keyval_bias, query_bias[cut:]])[None]
    rows_held = weights.shape[0]
    half = rows_held // 2
    order = lax.dynamic_index_in_dim(jnp.asarray(source_table()), own, 0, keepdims=False)
    widths = [count * rows_held for count in PIECES]
    gain = norm_gain[None]

    near = [first(weights, 1), first(weights, -1), first(weights, 2)]
    near += [second(weights, 1), second(weights, -1)]
    scale, x_near = norm(order, hidden_states, gain, widths[:1])
    near, scale, x_near, plan, bias = lax.optimization_barrier((near, scale, x_near, plan, bias))
    own_dest, own_length, source, joins = plan

    own_ahead, own_behind = near[3:]
    beside = jnp.concatenate(near[:3])
    ahead, behind = second(beside, 1), second(beside, -1)
    x_middle, x_corners, x_far, x_last = norm(
        order, hidden_states, gain, widths[1:], scale, widths[0] // half
    )
    straight = jnp.concatenate([weights, own_ahead, own_behind])
    total = project(None, x_near, [beside, straight])

    ahead, behind, straight, total, x_middle, x_corners, x_far, x_last = lax.optimization_barrier(
        (ahead, behind, straight, total, x_middle, x_corners, x_far, x_last)
    )
    far = [
        second(
            jnp.concatenate(
                [ahead[:rows_held], ahead[2 * rows_held : -half], straight[rows_held : rows_held + half]]
            ),
            1,
        ),
        second(
            jnp.concatenate(
                [behind[rows_held : 2 * rows_held], behind[-half:], straight[-half:]]
            ),
            -1,
        ),
    ]
    near = [swap(held_until(piece, ahead)) for piece in (beside, straight)]
    total = project(total, x_middle, [*near, ahead, behind])
    total = project(total, x_corners, [swap(ahead), swap(behind)])
    far, total = lax.optimization_barrier((far, total))
    last = [swap(piece) for piece in far]
    total = project(total, x_far, far)

    middle = cut + w_keyval.shape[1]
    given = (own_dest, own_length, total, x_last, bias)
    first_sent, keyval = attend(*given, None, last, packs, slice(0, middle))
    (second_sent,) = attend(*given, keyval, last, packs, slice(middle, weights.shape[1]))

    def exchanged(sent):
        received = lax.all_to_all(sent, "dp", split_axis=0, concat_axis=0, tiled=True)
        parts = place(source, received, planes)
        return [parts[0]] + [
            lax.ppermute(parts[k], "mp", [(i, (i + k) % planes) for i in range(planes)])
            for k in range(1, planes)
        ]

    columns = planes * w_query.shape[1]
    joined = join(joins, exchanged(first_sent), columns)
    return join(joins, exchanged(second_sent), columns, joined, cut)


def solution(mesh):
    return jax.shard_map(
        per_device,
        mesh=mesh,
        in_specs=(
            P("dp", None),
            P(),
            P("dp", "mp"),
            P("dp", "mp"),
            P("mp"),
            P("mp"),
            P(),
            P(),
            P(),
        ),
        out_specs=P(("dp", "mp"), None),
        check_vma=False,
    )
```

```python
import functools

import jax
import jax.numpy as jnp
import numpy as np
from jax import lax
from jax.experimental import pallas as pl
from jax.experimental.pallas import tpu as pltpu
from jax.sharding import PartitionSpec as P

HD = 128
GROUP = 64
SIDE = 4
MIB = 1024 * 1024
FIRST_HEADS = 6
PIECES = (6, 12, 6, 4, 4)

rope_base = 1000000.0
norm_epsilon = 1e-06


def rope_tables():
    half = HD // 2
    frequency = np.float32(rope_base) ** (
        -(np.arange(half, dtype=np.float32) * np.float32(2.0)) / np.float32(HD)
    )
    within = np.arange(GROUP)
    position = np.concatenate([within % length for length in (64, 32, 16, 8)])
    angles = position.astype(np.float32)[:, None] * frequency[None, :].astype(np.float32)
    cosine, sine = np.cos(angles), np.sin(angles)
    return (
        np.concatenate([cosine, cosine], 1).astype(np.float32),
        np.concatenate([-sine, sine], 1).astype(np.float32),
    )


def device_index(y, z, core):
    return ((y % SIDE) * SIDE + (z % SIDE)) * 2 + core


def shift_pairs(first, second):
    pairs = []
    for y in range(SIDE):
        for z in range(SIDE):
            pairs.append((device_index(y, z, 0), device_index(y + first, z + second, 0)))
            pairs.append((device_index(y, z, 1), device_index(y + second, z + first, 1)))
    return pairs


def swap_pairs():
    return [
        (device_index(y, z, core), device_index(y, z, 1 - core))
        for y in range(SIDE)
        for z in range(SIDE)
        for core in range(2)
    ]


def source_table():
    table = np.zeros((32, 64), np.int32)
    for y in range(SIDE):
        for z in range(SIDE):
            for core in range(2):

                def blocks(c, offsets):
                    found = []
                    for a, b, halves in offsets:
                        held = (
                            device_index(y - a, z - b, c)
                            if c == 0
                            else device_index(y - b, z - a, c)
                        )
                        found += [2 * held + half for half in halves]
                    return found

                both, low, high = (0, 1), (0,), (1,)
                near = [(1, 0, both), (3, 0, both), (2, 0, both)]
                near += [(0, 0, both), (0, 1, both), (0, 3, both)]
                corners = [(1, 1, both), (3, 1, both), (2, 1, both)]
                corners += [(1, 3, both), (3, 3, both), (2, 3, both)]
                far = [(1, 2, both), (2, 2, low), (0, 2, low)]
                far += [(3, 2, both), (2, 2, high), (0, 2, high)]
                order = []
                for offsets in (near, corners, far):
                    order += blocks(core, offsets) + blocks(1 - core, offsets)
                table[device_index(y, z, core)] = order
    return table


def beside_kernel(query_ref, keyval_ref, out_ref, sems):
    cut = FIRST_HEADS * HD
    middle = cut + keyval_ref.shape[1]
    copies = [
        pltpu.make_async_copy(
            query_ref.at[:, pl.ds(0, cut)], out_ref.at[:, pl.ds(0, cut)], sems.at[0]
        ),
        pltpu.make_async_copy(
            keyval_ref, out_ref.at[:, pl.ds(cut, middle - cut)], sems.at[1]
        ),
        pltpu.make_async_copy(
            query_ref.at[:, pl.ds(cut, query_ref.shape[1] - cut)],
            out_ref.at[:, pl.ds(middle, out_ref.shape[1] - middle)],
            sems.at[2],
        ),
    ]
    for copy in copies:
        copy.start()
    for copy in copies:
        copy.wait()


def side_by_side(w_query, w_keyval):
    rows = w_query.shape[0]
    return pl.pallas_call(
        beside_kernel,
        in_specs=[pl.BlockSpec(memory_space=pltpu.HBM)] * 2,
        out_specs=pl.BlockSpec(memory_space=pltpu.VMEM),
        out_shape=jax.ShapeDtypeStruct(
            (rows, w_query.shape[1] + w_keyval.shape[1]), w_query.dtype
        ),
        scratch_shapes=[pltpu.SemaphoreType.DMA((3,))],
        compiler_params=pltpu.CompilerParams(vmem_limit_bytes=58 * MIB),
        name="side_by_side",
    )(w_query, w_keyval)


def scaled_columns(order_ref, place, hidden_ref, gain_ref, scale, refs):
    depth = hidden_ref.shape[1] // order_ref.shape[0]
    for ref in refs:
        for j in range(ref.shape[1] // depth):
            start = pl.multiple_of(order_ref[place] * depth, depth)
            block = hidden_ref[:, pl.ds(start, depth)].astype(jnp.float32)
            gain = gain_ref[:, pl.ds(start, depth)]
            ref[:, j * depth : (j + 1) * depth] = (block * scale * gain).astype(jnp.bfloat16)
            place += 1


def norm_kernel(order_ref, hidden_ref, gain_ref, scale_ref, *refs):
    widened = hidden_ref[...].astype(jnp.float32)
    mean_square = jnp.sum(widened * widened, -1, keepdims=True) * (1.0 / widened.shape[1])
    scale = lax.rsqrt(mean_square + norm_epsilon)
    scale_ref[...] = scale
    scaled_columns(order_ref, 0, hidden_ref, gain_ref, scale, refs)


def norm_rest_kernel(place, order_ref, hidden_ref, gain_ref, scale_ref, *refs):
    scaled_columns(order_ref, place, hidden_ref, gain_ref, scale_ref[...], refs)


def norm(order, hidden, gain, widths, scale=None, place=0):
    rows, features = hidden.shape
    tile = 128
    given = [hidden, gain] + ([] if scale is None else [scale])
    in_specs = [
        pl.BlockSpec((tile, features), lambda i, order: (i, 0)),
        pl.BlockSpec((1, features), lambda i, order: (0, 0)),
    ]
    out_specs = [pl.BlockSpec((tile, w), lambda i, order: (i, 0)) for w in widths]
    out_shape = [pltpu.HBM((rows, w), jnp.bfloat16) for w in widths]
    scale_spec = pl.BlockSpec((tile, 1), lambda i, order: (i, 0))
    if scale is None:
        out_specs = [scale_spec] + out_specs
        out_shape = [jax.ShapeDtypeStruct((rows, 1), jnp.float32)] + out_shape
    else:
        in_specs = in_specs + [scale_spec]
    return pl.pallas_call(
        norm_kernel if scale is None else functools.partial(norm_rest_kernel, place),
        grid_spec=pltpu.PrefetchScalarGridSpec(
            num_scalar_prefetch=1, grid=(rows // tile,), in_specs=in_specs, out_specs=out_specs
        ),
        out_shape=out_shape,
        compiler_params=pltpu.CompilerParams(vmem_limit_bytes=18 * MIB),
        cost_estimate=pl.CostEstimate(
            flops=6 * rows * features,
            bytes_accessed=2 * rows * (features + sum(widths)),
            transcendentals=rows,
        ),
        name="norm",
    )(order, *given)


def product(x_ref, pieces, columns=slice(None)):
    weights = jnp.concatenate([piece[:, columns] for piece in pieces], axis=0)
    return jnp.dot(x_ref[...], weights, preferred_element_type=jnp.float32)


def tile_rows(tile):
    return pl.ds(pl.multiple_of(pl.program_id(0) * tile, tile), tile)


def first_kernel(x_ref, *refs):
    refs[-1][tile_rows(x_ref.shape[0]), :] = product(x_ref, refs[:-1])


def add_kernel(total_ref, x_ref, *refs):
    rows = tile_rows(x_ref.shape[0])
    refs[-1][rows, :] = total_ref[rows, :] + product(x_ref, refs[:-1])


def matmul_cost(rows, depth, columns, more):
    return pl.CostEstimate(
        flops=2 * rows * depth * columns,
        bytes_accessed=2 * depth * (rows + columns) + 4 * more * rows * columns,
        transcendentals=0,
    )


def project(total, x, pieces):
    rows, depth = x.shape
    columns = pieces[0].shape[1]
    tile = 256
    resident = pl.BlockSpec(memory_space=pltpu.VMEM)
    x_block = pl.BlockSpec((tile, depth), lambda i: (i, 0))
    totals = [] if total is None else [total]
    return pl.pallas_call(
        add_kernel if totals else first_kernel,
        grid=(rows // tile,),
        in_specs=[resident] * len(totals) + [x_block] + [resident] * len(pieces),
        out_specs=resident,
        out_shape=jax.ShapeDtypeStruct((rows, columns), jnp.float32),
        input_output_aliases={0: 0} if totals else {},
        compiler_params=pltpu.CompilerParams(vmem_limit_bytes=20 * MIB),
        cost_estimate=matmul_cost(rows, depth, columns, 2),
        name="project",
    )(*totals, x, *pieces)


def attend_kernel(
    columns, dest_ref, length_ref, total_ref, x_ref, bias_ref, cosine_ref, sine_ref, *refs
):
    makes_keyval = columns.start == 0
    if makes_keyval:
        pieces, (out_ref, keyval_ref, context, sems) = refs[:-4], refs[-4:]
    else:
        keyval_ref, pieces, (out_ref, context, sems) = refs[0], refs[1:-3], refs[-3:]
    rows = x_ref.shape[0]
    heads = context.shape[1] // HD
    groups = rows // GROUP

    lengths = [length_ref[g] for g in range(groups)]
    row_tables = []
    for table in (cosine_ref, sine_ref):
        parts = []
        for length in lengths:
            index = (
                (length < 64).astype(jnp.int32)
                + (length < 32).astype(jnp.int32)
                + (length < 16).astype(jnp.int32)
            )
            parts.append(table[pl.ds(pl.multiple_of(index * GROUP, GROUP), GROUP), :])
        row_tables.append(jnp.concatenate(parts, 0))
    cosine, sine = row_tables

    summed = (
        total_ref[:, columns]
        + product(x_ref, pieces, columns)
        + bias_ref[:, columns]
    )

    def rotated(column):
        head = summed[:, column : column + HD]
        return (head * cosine + pltpu.roll(head, HD // 2, 1) * sine).astype(jnp.bfloat16)

    query = [rotated(h * HD) for h in range(heads)]
    if makes_keyval:
        key = rotated(heads * HD)
        value = summed[:, (heads + 1) * HD :].astype(jnp.bfloat16)
        keyval_ref[:, :HD] = key
        keyval_ref[:, HD:] = value
    else:
        key, value = keyval_ref[:, :HD], keyval_ref[:, HD:]

    copies = []
    tile = 2 * GROUP
    row = lax.broadcasted_iota(jnp.int32, (tile, tile), 0)
    column = lax.broadcasted_iota(jnp.int32, (tile, tile), 1)
    for t in range(rows // tile):
        length = jnp.where(row < GROUP, lengths[2 * t], lengths[2 * t + 1])
        allowed = (column >= (row & -length)) & (column <= row)
        span = slice(t * tile, (t + 1) * tile)
        stacked = jnp.concatenate([q[span] for q in query], 0)
        scores = lax.dot_general(
            stacked, key[span], (((1,), (1,)), ((), ())), preferred_element_type=jnp.float32
        ) * (HD ** (-0.5))
        scores = jnp.where(allowed[None], scores.reshape(heads, tile, tile), -jnp.inf)
        weights = jnp.exp(scores - jnp.max(scores, -1, keepdims=True))
        weights = weights * (1.0 / jnp.sum(weights, -1, keepdims=True))
        weights = weights.astype(jnp.bfloat16).reshape(heads * tile, tile)
        mixed = jnp.dot(weights, value[span], preferred_element_type=jnp.float32)
        mixed = mixed.astype(jnp.bfloat16)
        for h in range(heads):
            context[span, h * HD : (h + 1) * HD] = mixed[h * tile : (h + 1) * tile]
        for g in (2 * t, 2 * t + 1):
            copy = pltpu.make_async_copy(
                context.at[pl.ds(g * GROUP, GROUP)], out_ref.at[dest_ref[g]], sems.at[g]
            )
            copy.start()
            copies.append(copy)
    for copy in copies:
        copy.wait()


def attend(dest, lengths, total, x, bias, keyval, pieces, packs, columns):
    rows, depth = x.shape
    cosine, sine = rope_tables()
    resident = pl.BlockSpec(memory_space=pltpu.VMEM)

    def fixed(shape):
        return pl.BlockSpec(
            shape, lambda i, *_: (0,) * len(shape), pipeline_mode=pl.Buffered(1)
        )

    def by_rows(width):
        return pl.BlockSpec((rows, width), lambda i, *_: (i, 0))

    width = columns.stop - columns.start
    out_specs = [pl.BlockSpec(memory_space=pltpu.HBM)]
    if keyval is None:
        width -= 2 * HD
        out_specs.append(by_rows(2 * HD))
    out_shape = [
        pltpu.HBM((packs, GROUP, width), jnp.bfloat16),
        jax.ShapeDtypeStruct((rows, 2 * HD), jnp.bfloat16),
    ]
    keyvals = [] if keyval is None else [keyval]
    return pl.pallas_call(
        functools.partial(attend_kernel, columns),
        grid_spec=pltpu.PrefetchScalarGridSpec(
            num_scalar_prefetch=2,
            grid=(1,),
            in_specs=[
                resident,
                by_rows(depth),
                fixed(bias.shape),
                fixed(cosine.shape),
                fixed(sine.shape),
            ]
            + [by_rows(2 * HD)] * len(keyvals)
            + [resident] * len(pieces),
            out_specs=out_specs,
            scratch_shapes=[
                pltpu.VMEM((rows, width), jnp.bfloat16),
                pltpu.SemaphoreType.DMA((rows // GROUP,)),
            ],
        ),
        out_shape=out_shape[: len(out_specs)],
        compiler_params=pltpu.CompilerParams(vmem_limit_bytes=28 * MIB),
        cost_estimate=matmul_cost(rows, depth, columns.stop - columns.start, 2),
        name="attend",
    )(dest, lengths, total, x, bias, cosine, sine, *keyvals, *pieces)


def place_kernel(source_ref, received_ref, *parts):
    per_part = parts[0].shape[0] // GROUP
    for k, part in enumerate(parts):
        for j in range(per_part):
            part[j * GROUP : (j + 1) * GROUP, :] = received_ref[source_ref[k * per_part + j]]


def place(source, received, parts):
    packs, group, width = received.shape
    per_part = source.shape[0] // parts
    resident = pl.BlockSpec(memory_space=pltpu.VMEM)
    return pl.pallas_call(
        place_kernel,
        grid_spec=pltpu.PrefetchScalarGridSpec(
            num_scalar_prefetch=1,
            grid=(1,),
            in_specs=[resident],
            out_specs=[resident] * parts,
        ),
        out_shape=[jax.ShapeDtypeStruct((per_part * group, width), received.dtype)] * parts,
        compiler_params=pltpu.CompilerParams(vmem_limit_bytes=8 * MIB),
        name="place",
    )(source, received)


def join_kernel(step, start, order_ref, *refs):
    parts, out_ref, sems = refs[:-2], refs[-2], refs[-1]
    if start > 0:
        parts = parts[1:]
    width = parts[0].shape[1]
    copies = []
    for k, part in enumerate(parts):
        column = pl.multiple_of(order_ref[k] * step + start, HD)
        copies.append(
            pltpu.make_async_copy(part, out_ref.at[:, pl.ds(column, width)], sems.at[k])
        )
    for copy in copies:
        copy.start()
    for copy in copies:
        copy.wait()


def join(order, parts, columns, joined=None, start=0):
    rows = parts[0].shape[0]
    whole = pl.BlockSpec(memory_space=pltpu.HBM)
    given = [] if joined is None else [joined]
    return pl.pallas_call(
        functools.partial(join_kernel, columns // len(parts), start),
        grid_spec=pltpu.PrefetchScalarGridSpec(
            num_scalar_prefetch=1,
            grid=(1,),
            in_specs=[whole] * len(given)
            + [pl.BlockSpec(memory_space=pltpu.VMEM)] * len(parts),
            out_specs=whole,
            scratch_shapes=[pltpu.SemaphoreType.DMA((len(parts),))],
        ),
        out_shape=jax.ShapeDtypeStruct((rows, columns), parts[0].dtype),
        input_output_aliases={1: 0} if given else {},
        compiler_params=pltpu.CompilerParams(vmem_limit_bytes=8 * MIB),
        name="join",
    )(order, *given, *parts)


def held_until(value, *others):
    return lax.optimization_barrier((value, *others))[0]


def per_device(
    hidden_states,
    norm_gain,
    w_query,
    w_keyval,
    query_bias,
    keyval_bias,
    group_dest,
    group_offset,
    group_length,
):
    own = lax.axis_index("dp")
    plane = lax.axis_index("mp")
    planes = lax.axis_size("mp")
    packs, groups = group_dest.shape
    rows, features = hidden_states.shape

    def first(piece, by):
        return lax.ppermute(piece, "dp", shift_pairs(by, 0))

    def second(piece, by):
        return lax.ppermute(piece, "dp", shift_pairs(0, by))

    def swap(piece):
        return lax.ppermute(piece, "dp", swap_pairs())

    own_dest = lax.dynamic_index_in_dim(group_dest, own, 0, keepdims=False)
    own_length = lax.dynamic_index_in_dim(group_length, own, 0, keepdims=False)
    slot = group_offset // GROUP
    hits = (group_dest == own)[None] & (
        slot[None] == jnp.arange(groups, dtype=jnp.int32)[:, None, None]
    )
    packs_of = jnp.arange(packs, dtype=jnp.int32)[None, :, None]
    source = jnp.sum(jnp.where(hits, packs_of, 0), (1, 2)).reshape(planes, -1)
    step = jnp.arange(planes, dtype=jnp.int32)
    source = source[(plane + step) % planes].reshape(-1)
    joins = (plane - jnp.array([0, 2, 1, 3], jnp.int32)) % planes
    plan = own_dest, own_length, source, joins

    cut = FIRST_HEADS * HD
    weights = side_by_side(w_query, w_keyval)
    bias = jnp.concatenate([query_bias[:cut], keyval_bias, query_bias[cut:]])[None]
    rows_held = weights.shape[0]
    half = rows_held // 2
    order = lax.dynamic_index_in_dim(jnp.asarray(source_table()), own, 0, keepdims=False)
    widths = [count * rows_held for count in PIECES]
    gain = norm_gain[None]

    near = [first(weights, 1), first(weights, -1), first(weights, 2)]
    near += [second(weights, 1), second(weights, -1)]
    scale, x_near = norm(order, hidden_states, gain, widths[:1])
    near, scale, x_near, plan, bias = lax.optimization_barrier((near, scale, x_near, plan, bias))
    own_dest, own_length, source, joins = plan

    own_ahead, own_behind = near[3:]
    beside = jnp.concatenate(near[:3])
    ahead, behind = second(beside, 1), second(beside, -1)
    x_middle, x_corners, x_far, x_last = norm(
        order, hidden_states, gain, widths[1:], scale, widths[0] // half
    )
    straight = jnp.concatenate([weights, own_ahead, own_behind])
    total = project(None, x_near, [beside, straight])

    ahead, behind, straight, total, x_middle, x_corners, x_far, x_last = lax.optimization_barrier(
        (ahead, behind, straight, total, x_middle, x_corners, x_far, x_last)
    )
    far = [
        second(
            jnp.concatenate(
                [ahead[:rows_held], ahead[2 * rows_held : -half], straight[rows_held : rows_held + half]]
            ),
            1,
        ),
        second(
            jnp.concatenate(
                [behind[rows_held : 2 * rows_held], behind[-half:], straight[-half:]]
            ),
            -1,
        ),
    ]
    near = [swap(held_until(piece, ahead)) for piece in (beside, straight)]
    total = project(total, x_middle, [*near, ahead, behind])
    total = project(total, x_corners, [swap(ahead), swap(behind)])
    far, total = lax.optimization_barrier((far, total))
    last = [swap(piece) for piece in far]
    total = project(total, x_far, far)

    middle = cut + w_keyval.shape[1]
    given = (own_dest, own_length, total, x_last, bias)
    first_sent, keyval = attend(*given, None, last, packs, slice(0, middle))
    (second_sent,) = attend(*given, keyval, last, packs, slice(middle, weights.shape[1]))

    def exchanged(sent):
        received = lax.all_to_all(sent, "dp", split_axis=0, concat_axis=0, tiled=True)
        parts = place(source, received, planes)
        return [parts[0]] + [
            lax.ppermute(parts[k], "mp", [(i, (i + k) % planes) for i in range(planes)])
            for k in (2, 1, 3)
        ]

    columns = planes * w_query.shape[1]
    joined = join(joins, exchanged(first_sent), columns)
    return join(joins, exchanged(second_sent), columns, joined, cut)


def solution(mesh):
    return jax.shard_map(
        per_device,
        mesh=mesh,
        in_specs=(
            P("dp", None),
            P(),
            P("dp", "mp"),
            P("dp", "mp"),
            P("mp"),
            P("mp"),
            P(),
            P(),
            P(),
        ),
        out_specs=P(("dp", "mp"), None),
        check_vma=False,
    )
```

```python
import functools

import jax
import jax.numpy as jnp
import numpy as np
from jax import lax
from jax.experimental import pallas as pl
from jax.experimental.pallas import tpu as pltpu
from jax.sharding import PartitionSpec as P

HD = 128
GROUP = 64
SIDE = 4
MIB = 1024 * 1024
FIRST_HEADS = 6
PIECES = (6, 6, 6, 6, 4, 4)

rope_base = 1000000.0
norm_epsilon = 1e-06


def rope_tables():
    half = HD // 2
    frequency = np.float32(rope_base) ** (
        -(np.arange(half, dtype=np.float32) * np.float32(2.0)) / np.float32(HD)
    )
    within = np.arange(GROUP)
    position = np.concatenate([within % length for length in (64, 32, 16, 8)])
    angles = position.astype(np.float32)[:, None] * frequency[None, :].astype(np.float32)
    cosine, sine = np.cos(angles), np.sin(angles)
    return (
        np.concatenate([cosine, cosine], 1).astype(np.float32),
        np.concatenate([-sine, sine], 1).astype(np.float32),
    )


def device_index(y, z, core):
    return ((y % SIDE) * SIDE + (z % SIDE)) * 2 + core


def shift_pairs(first, second):
    pairs = []
    for y in range(SIDE):
        for z in range(SIDE):
            pairs.append((device_index(y, z, 0), device_index(y + first, z + second, 0)))
            pairs.append((device_index(y, z, 1), device_index(y + second, z + first, 1)))
    return pairs


def swap_pairs():
    return [
        (device_index(y, z, core), device_index(y, z, 1 - core))
        for y in range(SIDE)
        for z in range(SIDE)
        for core in range(2)
    ]


def source_table():
    table = np.zeros((32, 64), np.int32)
    for y in range(SIDE):
        for z in range(SIDE):
            for core in range(2):

                def blocks(c, offsets):
                    found = []
                    for a, b, halves in offsets:
                        held = (
                            device_index(y - a, z - b, c)
                            if c == 0
                            else device_index(y - b, z - a, c)
                        )
                        found += [2 * held + half for half in halves]
                    return found

                both, low, high = (0, 1), (0,), (1,)
                near = [(1, 0, both), (3, 0, both), (2, 0, both)]
                near += [(0, 0, both), (0, 1, both), (0, 3, both)]
                corners = [(1, 1, both), (3, 1, both), (2, 1, both)]
                corners += [(1, 3, both), (3, 3, both), (2, 3, both)]
                far = [(3, 2, both), (2, 2, high), (0, 2, high)]
                far += [(1, 2, both), (2, 2, low), (0, 2, low)]
                order = []
                for offsets in (near, corners, far):
                    order += blocks(core, offsets) + blocks(1 - core, offsets)
                table[device_index(y, z, core)] = order
    return table


def beside_kernel(query_ref, keyval_ref, out_ref, sems):
    cut = FIRST_HEADS * HD
    middle = cut + keyval_ref.shape[1]
    copies = [
        pltpu.make_async_copy(
            query_ref.at[:, pl.ds(0, cut)], out_ref.at[:, pl.ds(0, cut)], sems.at[0]
        ),
        pltpu.make_async_copy(
            keyval_ref, out_ref.at[:, pl.ds(cut, middle - cut)], sems.at[1]
        ),
        pltpu.make_async_copy(
            query_ref.at[:, pl.ds(cut, query_ref.shape[1] - cut)],
            out_ref.at[:, pl.ds(middle, out_ref.shape[1] - middle)],
            sems.at[2],
        ),
    ]
    for copy in copies:
        copy.start()
    for copy in copies:
        copy.wait()


def side_by_side(w_query, w_keyval):
    rows = w_query.shape[0]
    return pl.pallas_call(
        beside_kernel,
        in_specs=[pl.BlockSpec(memory_space=pltpu.HBM)] * 2,
        out_specs=pl.BlockSpec(memory_space=pltpu.VMEM),
        out_shape=jax.ShapeDtypeStruct(
            (rows, w_query.shape[1] + w_keyval.shape[1]), w_query.dtype
        ),
        scratch_shapes=[pltpu.SemaphoreType.DMA((3,))],
        compiler_params=pltpu.CompilerParams(vmem_limit_bytes=58 * MIB),
        name="side_by_side",
    )(w_query, w_keyval)


def scaled_columns(order_ref, place, hidden_ref, gain_ref, scale, refs):
    depth = hidden_ref.shape[1] // order_ref.shape[0]
    for ref in refs:
        for j in range(ref.shape[1] // depth):
            start = pl.multiple_of(order_ref[place] * depth, depth)
            block = hidden_ref[:, pl.ds(start, depth)].astype(jnp.float32)
            gain = gain_ref[:, pl.ds(start, depth)]
            ref[:, j * depth : (j + 1) * depth] = (block * scale * gain).astype(jnp.bfloat16)
            place += 1


def norm_kernel(order_ref, hidden_ref, gain_ref, scale_ref, *refs):
    widened = hidden_ref[...].astype(jnp.float32)
    mean_square = jnp.sum(widened * widened, -1, keepdims=True) * (1.0 / widened.shape[1])
    scale = lax.rsqrt(mean_square + norm_epsilon)
    scale_ref[...] = scale
    scaled_columns(order_ref, 0, hidden_ref, gain_ref, scale, refs)


def norm_rest_kernel(place, order_ref, hidden_ref, gain_ref, scale_ref, *refs):
    scaled_columns(order_ref, place, hidden_ref, gain_ref, scale_ref[...], refs)


def norm(order, hidden, gain, widths, scale=None, place=0):
    rows, features = hidden.shape
    tile = 128
    given = [hidden, gain] + ([] if scale is None else [scale])
    in_specs = [
        pl.BlockSpec((tile, features), lambda i, order: (i, 0)),
        pl.BlockSpec((1, features), lambda i, order: (0, 0)),
    ]
    out_specs = [pl.BlockSpec((tile, w), lambda i, order: (i, 0)) for w in widths]
    out_shape = [pltpu.HBM((rows, w), jnp.bfloat16) for w in widths]
    scale_spec = pl.BlockSpec((tile, 1), lambda i, order: (i, 0))
    if scale is None:
        out_specs = [scale_spec] + out_specs
        out_shape = [jax.ShapeDtypeStruct((rows, 1), jnp.float32)] + out_shape
    else:
        in_specs = in_specs + [scale_spec]
    return pl.pallas_call(
        norm_kernel if scale is None else functools.partial(norm_rest_kernel, place),
        grid_spec=pltpu.PrefetchScalarGridSpec(
            num_scalar_prefetch=1, grid=(rows // tile,), in_specs=in_specs, out_specs=out_specs
        ),
        out_shape=out_shape,
        compiler_params=pltpu.CompilerParams(vmem_limit_bytes=18 * MIB),
        cost_estimate=pl.CostEstimate(
            flops=6 * rows * features,
            bytes_accessed=2 * rows * (features + sum(widths)),
            transcendentals=rows,
        ),
        name="norm",
    )(order, *given)


def product(x_ref, pieces, columns=slice(None)):
    weights = jnp.concatenate([piece[:, columns] for piece in pieces], axis=0)
    return jnp.dot(x_ref[...], weights, preferred_element_type=jnp.float32)


def tile_rows(tile):
    return pl.ds(pl.multiple_of(pl.program_id(0) * tile, tile), tile)


def first_kernel(x_ref, *refs):
    refs[-1][tile_rows(x_ref.shape[0]), :] = product(x_ref, refs[:-1])


def add_kernel(total_ref, x_ref, *refs):
    rows = tile_rows(x_ref.shape[0])
    refs[-1][rows, :] = total_ref[rows, :] + product(x_ref, refs[:-1])


def matmul_cost(rows, depth, columns, more):
    return pl.CostEstimate(
        flops=2 * rows * depth * columns,
        bytes_accessed=2 * depth * (rows + columns) + 4 * more * rows * columns,
        transcendentals=0,
    )


SHORT = pl.CostEstimate(flops=1024, bytes_accessed=1024, transcendentals=0)


def project(total, x, pieces, cost=None):
    rows, depth = x.shape
    columns = pieces[0].shape[1]
    tile = 256
    resident = pl.BlockSpec(memory_space=pltpu.VMEM)
    x_block = pl.BlockSpec((tile, depth), lambda i: (i, 0))
    totals = [] if total is None else [total]
    return pl.pallas_call(
        add_kernel if totals else first_kernel,
        grid=(rows // tile,),
        in_specs=[resident] * len(totals) + [x_block] + [resident] * len(pieces),
        out_specs=resident,
        out_shape=jax.ShapeDtypeStruct((rows, columns), jnp.float32),
        input_output_aliases={0: 0} if totals else {},
        compiler_params=pltpu.CompilerParams(vmem_limit_bytes=20 * MIB),
        cost_estimate=cost or matmul_cost(rows, depth, columns, 2),
        name="project",
    )(*totals, x, *pieces)


def attend_kernel(
    columns, dest_ref, length_ref, total_ref, x_ref, bias_ref, cosine_ref, sine_ref, *refs
):
    makes_keyval = columns.start == 0
    if makes_keyval:
        pieces, (out_ref, keyval_ref, context, sems) = refs[:-4], refs[-4:]
    else:
        keyval_ref, pieces, (out_ref, context, sems) = refs[0], refs[1:-3], refs[-3:]
    rows = x_ref.shape[0]
    heads = context.shape[1] // HD
    groups = rows // GROUP

    lengths = [length_ref[g] for g in range(groups)]
    row_tables = []
    for table in (cosine_ref, sine_ref):
        parts = []
        for length in lengths:
            index = (
                (length < 64).astype(jnp.int32)
                + (length < 32).astype(jnp.int32)
                + (length < 16).astype(jnp.int32)
            )
            parts.append(table[pl.ds(pl.multiple_of(index * GROUP, GROUP), GROUP), :])
        row_tables.append(jnp.concatenate(parts, 0))
    cosine, sine = row_tables

    summed = (
        total_ref[:, columns]
        + product(x_ref, pieces, columns)
        + bias_ref[:, columns]
    )

    def rotated(column):
        head = summed[:, column : column + HD]
        return (head * cosine + pltpu.roll(head, HD // 2, 1) * sine).astype(jnp.bfloat16)

    query = [rotated(h * HD) for h in range(heads)]
    if makes_keyval:
        key = rotated(heads * HD)
        value = summed[:, (heads + 1) * HD :].astype(jnp.bfloat16)
        keyval_ref[:, :HD] = key
        keyval_ref[:, HD:] = value
    else:
        key, value = keyval_ref[:, :HD], keyval_ref[:, HD:]

    copies = []
    tile = 2 * GROUP
    row = lax.broadcasted_iota(jnp.int32, (tile, tile), 0)
    column = lax.broadcasted_iota(jnp.int32, (tile, tile), 1)
    for t in range(rows // tile):
        length = jnp.where(row < GROUP, lengths[2 * t], lengths[2 * t + 1])
        allowed = (column >= (row & -length)) & (column <= row)
        span = slice(t * tile, (t + 1) * tile)
        stacked = jnp.concatenate([q[span] for q in query], 0)
        scores = lax.dot_general(
            stacked, key[span], (((1,), (1,)), ((), ())), preferred_element_type=jnp.float32
        ) * (HD ** (-0.5))
        scores = jnp.where(allowed[None], scores.reshape(heads, tile, tile), -jnp.inf)
        weights = jnp.exp(scores - jnp.max(scores, -1, keepdims=True))
        weights = weights * (1.0 / jnp.sum(weights, -1, keepdims=True))
        weights = weights.astype(jnp.bfloat16).reshape(heads * tile, tile)
        mixed = jnp.dot(weights, value[span], preferred_element_type=jnp.float32)
        mixed = mixed.astype(jnp.bfloat16)
        for h in range(heads):
            context[span, h * HD : (h + 1) * HD] = mixed[h * tile : (h + 1) * tile]
        for g in (2 * t, 2 * t + 1):
            copy = pltpu.make_async_copy(
                context.at[pl.ds(g * GROUP, GROUP)], out_ref.at[dest_ref[g]], sems.at[g]
            )
            copy.start()
            copies.append(copy)
    for copy in copies:
        copy.wait()


def attend(dest, lengths, total, x, bias, keyval, pieces, packs, columns):
    rows, depth = x.shape
    cosine, sine = rope_tables()
    resident = pl.BlockSpec(memory_space=pltpu.VMEM)

    def fixed(shape):
        return pl.BlockSpec(
            shape, lambda i, *_: (0,) * len(shape), pipeline_mode=pl.Buffered(1)
        )

    def by_rows(width):
        return pl.BlockSpec((rows, width), lambda i, *_: (i, 0))

    width = columns.stop - columns.start
    out_specs = [pl.BlockSpec(memory_space=pltpu.HBM)]
    if keyval is None:
        width -= 2 * HD
        out_specs.append(by_rows(2 * HD))
    out_shape = [
        pltpu.HBM((packs, GROUP, width), jnp.bfloat16),
        jax.ShapeDtypeStruct((rows, 2 * HD), jnp.bfloat16),
    ]
    keyvals = [] if keyval is None else [keyval]
    return pl.pallas_call(
        functools.partial(attend_kernel, columns),
        grid_spec=pltpu.PrefetchScalarGridSpec(
            num_scalar_prefetch=2,
            grid=(1,),
            in_specs=[
                resident,
                by_rows(depth),
                fixed(bias.shape),
                fixed(cosine.shape),
                fixed(sine.shape),
            ]
            + [by_rows(2 * HD)] * len(keyvals)
            + [resident] * len(pieces),
            out_specs=out_specs,
            scratch_shapes=[
                pltpu.VMEM((rows, width), jnp.bfloat16),
                pltpu.SemaphoreType.DMA((rows // GROUP,)),
            ],
        ),
        out_shape=out_shape[: len(out_specs)],
        compiler_params=pltpu.CompilerParams(vmem_limit_bytes=28 * MIB),
        cost_estimate=matmul_cost(rows, depth, columns.stop - columns.start, 2),
        name="attend",
    )(dest, lengths, total, x, bias, cosine, sine, *keyvals, *pieces)


def place_kernel(source_ref, received_ref, *parts):
    per_part = parts[0].shape[0] // GROUP
    for k, part in enumerate(parts):
        for j in range(per_part):
            part[j * GROUP : (j + 1) * GROUP, :] = received_ref[source_ref[k * per_part + j]]


def place(source, received, parts):
    packs, group, width = received.shape
    per_part = source.shape[0] // parts
    resident = pl.BlockSpec(memory_space=pltpu.VMEM)
    return pl.pallas_call(
        place_kernel,
        grid_spec=pltpu.PrefetchScalarGridSpec(
            num_scalar_prefetch=1,
            grid=(1,),
            in_specs=[resident],
            out_specs=[resident] * parts,
        ),
        out_shape=[jax.ShapeDtypeStruct((per_part * group, width), received.dtype)] * parts,
        compiler_params=pltpu.CompilerParams(vmem_limit_bytes=8 * MIB),
        name="place",
    )(source, received)


def join_kernel(step, start, order_ref, *refs):
    parts, out_ref, sems = refs[:-2], refs[-2], refs[-1]
    if start > 0:
        parts = parts[1:]
    width = parts[0].shape[1]
    copies = []
    for k, part in enumerate(parts):
        column = pl.multiple_of(order_ref[k] * step + start, HD)
        copies.append(
            pltpu.make_async_copy(part, out_ref.at[:, pl.ds(column, width)], sems.at[k])
        )
    for copy in copies:
        copy.start()
    for copy in copies:
        copy.wait()


def join(order, parts, columns, joined=None, start=0):
    rows = parts[0].shape[0]
    whole = pl.BlockSpec(memory_space=pltpu.HBM)
    given = [] if joined is None else [joined]
    return pl.pallas_call(
        functools.partial(join_kernel, columns // len(parts), start),
        grid_spec=pltpu.PrefetchScalarGridSpec(
            num_scalar_prefetch=1,
            grid=(1,),
            in_specs=[whole] * len(given)
            + [pl.BlockSpec(memory_space=pltpu.VMEM)] * len(parts),
            out_specs=whole,
            scratch_shapes=[pltpu.SemaphoreType.DMA((len(parts),))],
        ),
        out_shape=jax.ShapeDtypeStruct((rows, columns), parts[0].dtype),
        input_output_aliases={1: 0} if given else {},
        compiler_params=pltpu.CompilerParams(vmem_limit_bytes=8 * MIB),
        name="join",
    )(order, *given, *parts)


def held_until(value, *others):
    return lax.optimization_barrier((value, *others))[0]


def per_device(
    hidden_states,
    norm_gain,
    w_query,
    w_keyval,
    query_bias,
    keyval_bias,
    group_dest,
    group_offset,
    group_length,
):
    own = lax.axis_index("dp")
    plane = lax.axis_index("mp")
    planes = lax.axis_size("mp")
    packs, groups = group_dest.shape
    rows, features = hidden_states.shape

    def first(piece, by):
        return lax.ppermute(piece, "dp", shift_pairs(by, 0))

    def second(piece, by):
        return lax.ppermute(piece, "dp", shift_pairs(0, by))

    def swap(piece):
        return lax.ppermute(piece, "dp", swap_pairs())

    own_dest = lax.dynamic_index_in_dim(group_dest, own, 0, keepdims=False)
    own_length = lax.dynamic_index_in_dim(group_length, own, 0, keepdims=False)
    slot = group_offset // GROUP
    hits = (group_dest == own)[None] & (
        slot[None] == jnp.arange(groups, dtype=jnp.int32)[:, None, None]
    )
    packs_of = jnp.arange(packs, dtype=jnp.int32)[None, :, None]
    source = jnp.sum(jnp.where(hits, packs_of, 0), (1, 2)).reshape(planes, -1)
    step = jnp.arange(planes, dtype=jnp.int32)
    source = source[(plane + step) % planes].reshape(-1)
    joins = (plane - jnp.array([0, 2, 1, 3], jnp.int32)) % planes
    plan = own_dest, own_length, source, joins

    cut = FIRST_HEADS * HD
    weights = side_by_side(w_query, w_keyval)
    bias = jnp.concatenate([query_bias[:cut], keyval_bias, query_bias[cut:]])[None]
    rows_held = weights.shape[0]
    half = rows_held // 2
    order = lax.dynamic_index_in_dim(jnp.asarray(source_table()), own, 0, keepdims=False)
    widths = [count * rows_held for count in PIECES]
    gain = norm_gain[None]

    near = [first(weights, 1), first(weights, -1), first(weights, 2)]
    near += [second(weights, 1), second(weights, -1)]
    scale, x_near = norm(order, hidden_states, gain, widths[:1])
    near, scale, x_near, plan, bias = lax.optimization_barrier((near, scale, x_near, plan, bias))
    own_dest, own_length, source, joins = plan

    own_ahead, own_behind = near[3:]
    beside = jnp.concatenate(near[:3])
    ahead, behind = second(beside, 1), second(beside, -1)
    x_middle, x_corners, x_swapped, x_far, x_last = norm(
        order, hidden_states, gain, widths[1:], scale, widths[0] // half
    )
    straight = jnp.concatenate([weights, own_ahead, own_behind])
    total = project(None, x_near, [beside, straight])
    pairs = [beside[: 2 * rows_held], jnp.concatenate([near[2], weights]), straight[rows_held:]]
    pairs = [swap(held_until(piece, total)) for piece in pairs]
    total = project(total, x_middle, pairs, SHORT)

    ahead, behind, straight, total, x_corners, x_swapped, x_far, x_last = lax.optimization_barrier(
        (ahead, behind, straight, total, x_corners, x_swapped, x_far, x_last)
    )
    far = [
        second(
            jnp.concatenate(
                [behind[rows_held : 2 * rows_held], behind[-half:], straight[-half:]]
            ),
            -1,
        ),
        second(
            jnp.concatenate(
                [
                    ahead[:rows_held],
                    ahead[2 * rows_held : -half],
                    straight[rows_held : rows_held + half],
                ]
            ),
            1,
        ),
    ]
    total = project(total, x_corners, [ahead, behind])
    total = project(total, x_swapped, [swap(ahead), swap(behind)])
    far, total = lax.optimization_barrier((far, total))
    last = [swap(piece) for piece in far]
    total = project(total, x_far, far)

    middle = cut + w_keyval.shape[1]
    given = (own_dest, own_length, total, x_last, bias)
    first_sent, keyval = attend(*given, None, last, packs, slice(0, middle))
    (second_sent,) = attend(*given, keyval, last, packs, slice(middle, weights.shape[1]))

    def exchanged(sent):
        received = lax.all_to_all(sent, "dp", split_axis=0, concat_axis=0, tiled=True)
        parts = place(source, received, planes)
        return [parts[0]] + [
            lax.ppermute(parts[k], "mp", [(i, (i + k) % planes) for i in range(planes)])
            for k in (2, 1, 3)
        ]

    columns = planes * w_query.shape[1]
    joined = join(joins, exchanged(first_sent), columns)
    return join(joins, exchanged(second_sent), columns, joined, cut)


def solution(mesh):
    return jax.shard_map(
        per_device,
        mesh=mesh,
        in_specs=(
            P("dp", None),
            P(),
            P("dp", "mp"),
            P("dp", "mp"),
            P("mp"),
            P("mp"),
            P(),
            P(),
            P(),
        ),
        out_specs=P(("dp", "mp"), None),
        check_vma=False,
    )
```

```python
import functools

import jax
import jax.numpy as jnp
import numpy as np
from jax import lax
from jax.experimental import pallas as pl
from jax.experimental.pallas import tpu as pltpu
from jax.sharding import PartitionSpec as P

HD = 128
GROUP = 64
SIDE = 4
MIB = 1024 * 1024
FIRST_HEADS = 6
PIECES = (6, 6, 6, 6, 4, 4)

rope_base = 1000000.0
norm_epsilon = 1e-06


def rope_tables():
    half = HD // 2
    frequency = np.float32(rope_base) ** (
        -(np.arange(half, dtype=np.float32) * np.float32(2.0)) / np.float32(HD)
    )
    within = np.arange(GROUP)
    position = np.concatenate([within % length for length in (64, 32, 16, 8)])
    angles = position.astype(np.float32)[:, None] * frequency[None, :].astype(np.float32)
    cosine, sine = np.cos(angles), np.sin(angles)
    return (
        np.concatenate([cosine, cosine], 1).astype(np.float32),
        np.concatenate([-sine, sine], 1).astype(np.float32),
    )


def device_index(y, z, core):
    return ((y % SIDE) * SIDE + (z % SIDE)) * 2 + core


def shift_pairs(first, second):
    pairs = []
    for y in range(SIDE):
        for z in range(SIDE):
            pairs.append((device_index(y, z, 0), device_index(y + first, z + second, 0)))
            pairs.append((device_index(y, z, 1), device_index(y + second, z + first, 1)))
    return pairs


def swap_pairs():
    return [
        (device_index(y, z, core), device_index(y, z, 1 - core))
        for y in range(SIDE)
        for z in range(SIDE)
        for core in range(2)
    ]


def source_table():
    table = np.zeros((32, 64), np.int32)
    for y in range(SIDE):
        for z in range(SIDE):
            for core in range(2):

                def blocks(c, offsets):
                    found = []
                    for a, b, halves in offsets:
                        held = (
                            device_index(y - a, z - b, c)
                            if c == 0
                            else device_index(y - b, z - a, c)
                        )
                        found += [2 * held + half for half in halves]
                    return found

                both, low, high = (0, 1), (0,), (1,)
                near = [(1, 0, both), (3, 0, both), (2, 0, both)]
                near += [(0, 0, both), (0, 1, both), (0, 3, both)]
                corners = [(1, 1, both), (3, 1, both), (2, 1, both)]
                corners += [(1, 3, both), (3, 3, both), (2, 3, both)]
                far = [(3, 2, both), (2, 2, high), (0, 2, high)]
                far += [(1, 2, both), (2, 2, low), (0, 2, low)]
                order = []
                for offsets in (near, corners, far):
                    order += blocks(core, offsets) + blocks(1 - core, offsets)
                table[device_index(y, z, core)] = order
    return table


def beside_kernel(query_ref, keyval_ref, out_ref, sems):
    cut = FIRST_HEADS * HD
    middle = cut + keyval_ref.shape[1]
    copies = [
        pltpu.make_async_copy(
            query_ref.at[:, pl.ds(0, cut)], out_ref.at[:, pl.ds(0, cut)], sems.at[0]
        ),
        pltpu.make_async_copy(
            keyval_ref, out_ref.at[:, pl.ds(cut, middle - cut)], sems.at[1]
        ),
        pltpu.make_async_copy(
            query_ref.at[:, pl.ds(cut, query_ref.shape[1] - cut)],
            out_ref.at[:, pl.ds(middle, out_ref.shape[1] - middle)],
            sems.at[2],
        ),
    ]
    for copy in copies:
        copy.start()
    for copy in copies:
        copy.wait()


def side_by_side(w_query, w_keyval):
    rows = w_query.shape[0]
    return pl.pallas_call(
        beside_kernel,
        in_specs=[pl.BlockSpec(memory_space=pltpu.HBM)] * 2,
        out_specs=pl.BlockSpec(memory_space=pltpu.VMEM),
        out_shape=jax.ShapeDtypeStruct(
            (rows, w_query.shape[1] + w_keyval.shape[1]), w_query.dtype
        ),
        scratch_shapes=[pltpu.SemaphoreType.DMA((3,))],
        compiler_params=pltpu.CompilerParams(vmem_limit_bytes=58 * MIB),
        name="side_by_side",
    )(w_query, w_keyval)


def scaled_columns(order_ref, place, hidden_ref, gain_ref, scale, refs):
    depth = hidden_ref.shape[1] // order_ref.shape[0]
    for ref in refs:
        for j in range(ref.shape[1] // depth):
            start = pl.multiple_of(order_ref[place] * depth, depth)
            block = hidden_ref[:, pl.ds(start, depth)].astype(jnp.float32)
            gain = gain_ref[:, pl.ds(start, depth)]
            ref[:, j * depth : (j + 1) * depth] = (block * scale * gain).astype(jnp.bfloat16)
            place += 1


def norm_kernel(order_ref, hidden_ref, gain_ref, scale_ref, *refs):
    widened = hidden_ref[...].astype(jnp.float32)
    mean_square = jnp.sum(widened * widened, -1, keepdims=True) * (1.0 / widened.shape[1])
    scale = lax.rsqrt(mean_square + norm_epsilon)
    scale_ref[...] = scale
    scaled_columns(order_ref, 0, hidden_ref, gain_ref, scale, refs)


def norm_rest_kernel(place, order_ref, hidden_ref, gain_ref, scale_ref, *refs):
    scaled_columns(order_ref, place, hidden_ref, gain_ref, scale_ref[...], refs)


def norm(order, hidden, gain, widths, scale=None, place=0):
    rows, features = hidden.shape
    tile = 128
    given = [hidden, gain] + ([] if scale is None else [scale])
    in_specs = [
        pl.BlockSpec((tile, features), lambda i, order: (i, 0)),
        pl.BlockSpec((1, features), lambda i, order: (0, 0)),
    ]
    out_specs = [pl.BlockSpec((tile, w), lambda i, order: (i, 0)) for w in widths]
    out_shape = [pltpu.HBM((rows, w), jnp.bfloat16) for w in widths]
    scale_spec = pl.BlockSpec((tile, 1), lambda i, order: (i, 0))
    if scale is None:
        out_specs = [scale_spec] + out_specs
        out_shape = [jax.ShapeDtypeStruct((rows, 1), jnp.float32)] + out_shape
    else:
        in_specs = in_specs + [scale_spec]
    return pl.pallas_call(
        norm_kernel if scale is None else functools.partial(norm_rest_kernel, place),
        grid_spec=pltpu.PrefetchScalarGridSpec(
            num_scalar_prefetch=1, grid=(rows // tile,), in_specs=in_specs, out_specs=out_specs
        ),
        out_shape=out_shape,
        compiler_params=pltpu.CompilerParams(vmem_limit_bytes=18 * MIB),
        cost_estimate=pl.CostEstimate(
            flops=6 * rows * features,
            bytes_accessed=2 * rows * (features + sum(widths)),
            transcendentals=rows,
        ),
        name="norm",
    )(order, *given)


def product(x_ref, pieces):
    weights = jnp.concatenate([piece[...] for piece in pieces], axis=0)
    return jnp.dot(x_ref[...], weights, preferred_element_type=jnp.float32)


def tile_rows(tile):
    return pl.ds(pl.multiple_of(pl.program_id(0) * tile, tile), tile)


def first_kernel(x_ref, *refs):
    refs[-1][tile_rows(x_ref.shape[0]), :] = product(x_ref, refs[:-1])


def add_kernel(total_ref, x_ref, *refs):
    rows = tile_rows(x_ref.shape[0])
    refs[-1][rows, :] = total_ref[rows, :] + product(x_ref, refs[:-1])


def matmul_cost(rows, depth, columns, more):
    return pl.CostEstimate(
        flops=2 * rows * depth * columns,
        bytes_accessed=2 * depth * (rows + columns) + 4 * more * rows * columns,
        transcendentals=0,
    )


SHORT = pl.CostEstimate(flops=1024, bytes_accessed=1024, transcendentals=0)


def project(total, x, pieces, cost=None):
    rows, depth = x.shape
    columns = pieces[0].shape[1]
    tile = 512
    resident = pl.BlockSpec(memory_space=pltpu.VMEM)
    x_block = pl.BlockSpec((tile, depth), lambda i: (i, 0))
    totals = [] if total is None else [total]
    return pl.pallas_call(
        add_kernel if totals else first_kernel,
        grid=(rows // tile,),
        in_specs=[resident] * len(totals) + [x_block] + [resident] * len(pieces),
        out_specs=resident,
        out_shape=jax.ShapeDtypeStruct((rows, columns), jnp.float32),
        input_output_aliases={0: 0} if totals else {},
        compiler_params=pltpu.CompilerParams(vmem_limit_bytes=20 * MIB),
        cost_estimate=cost or matmul_cost(rows, depth, columns, 2),
        name="project",
    )(*totals, x, *pieces)


def attend_kernel(
    columns, dest_ref, length_ref, total_ref, x_ref, bias_ref, cosine_ref, sine_ref, *refs
):
    makes_keyval = columns.start == 0
    if makes_keyval:
        pieces, (out_ref, keyval_ref, context, sems) = refs[:-4], refs[-4:]
    else:
        keyval_ref, pieces, (out_ref, context, sems) = refs[0], refs[1:-3], refs[-3:]
    rows = x_ref.shape[0]
    heads = context.shape[1] // HD
    groups = rows // GROUP

    lengths = [length_ref[g] for g in range(groups)]
    row_tables = []
    for table in (cosine_ref, sine_ref):
        parts = []
        for length in lengths:
            index = (
                (length < 64).astype(jnp.int32)
                + (length < 32).astype(jnp.int32)
                + (length < 16).astype(jnp.int32)
            )
            parts.append(table[pl.ds(pl.multiple_of(index * GROUP, GROUP), GROUP), :])
        row_tables.append(jnp.concatenate(parts, 0))
    cosine, sine = row_tables

    summed = (
        total_ref[:, columns]
        + product(x_ref, pieces)
        + bias_ref[:, columns]
    )

    def rotated(column):
        head = summed[:, column : column + HD]
        return (head * cosine + pltpu.roll(head, HD // 2, 1) * sine).astype(jnp.bfloat16)

    query = [rotated(h * HD) for h in range(heads)]
    if makes_keyval:
        key = rotated(heads * HD)
        value = summed[:, (heads + 1) * HD :].astype(jnp.bfloat16)
        keyval_ref[:, :HD] = key
        keyval_ref[:, HD:] = value
    else:
        key, value = keyval_ref[:, :HD], keyval_ref[:, HD:]

    copies = []
    tile = 2 * GROUP
    row = lax.broadcasted_iota(jnp.int32, (tile, tile), 0)
    column = lax.broadcasted_iota(jnp.int32, (tile, tile), 1)
    for t in range(rows // tile):
        length = jnp.where(row < GROUP, lengths[2 * t], lengths[2 * t + 1])
        allowed = (column >= (row & -length)) & (column <= row)
        span = slice(t * tile, (t + 1) * tile)
        stacked = jnp.concatenate([q[span] for q in query], 0)
        scores = lax.dot_general(
            stacked, key[span], (((1,), (1,)), ((), ())), preferred_element_type=jnp.float32
        ) * (HD ** (-0.5))
        scores = jnp.where(allowed[None], scores.reshape(heads, tile, tile), -jnp.inf)
        weights = jnp.exp(scores - jnp.max(scores, -1, keepdims=True))
        weights = weights * (1.0 / jnp.sum(weights, -1, keepdims=True))
        weights = weights.astype(jnp.bfloat16).reshape(heads * tile, tile)
        mixed = jnp.dot(weights, value[span], preferred_element_type=jnp.float32)
        mixed = mixed.astype(jnp.bfloat16)
        for h in range(heads):
            context[span, h * HD : (h + 1) * HD] = mixed[h * tile : (h + 1) * tile]
        for g in (2 * t, 2 * t + 1):
            copy = pltpu.make_async_copy(
                context.at[pl.ds(g * GROUP, GROUP)], out_ref.at[dest_ref[g]], sems.at[g]
            )
            copy.start()
            copies.append(copy)
    for copy in copies:
        copy.wait()


def attend(dest, lengths, total, x, bias, keyval, pieces, packs, columns):
    rows, depth = x.shape
    cosine, sine = rope_tables()
    resident = pl.BlockSpec(memory_space=pltpu.VMEM)

    def fixed(shape):
        return pl.BlockSpec(
            shape, lambda i, *_: (0,) * len(shape), pipeline_mode=pl.Buffered(1)
        )

    def by_rows(width):
        return pl.BlockSpec((rows, width), lambda i, *_: (i, 0))

    width = columns.stop - columns.start
    out_specs = [pl.BlockSpec(memory_space=pltpu.HBM)]
    if keyval is None:
        width -= 2 * HD
        out_specs.append(by_rows(2 * HD))
    out_shape = [
        pltpu.HBM((packs, GROUP, width), jnp.bfloat16),
        jax.ShapeDtypeStruct((rows, 2 * HD), jnp.bfloat16),
    ]
    keyvals = [] if keyval is None else [keyval]
    return pl.pallas_call(
        functools.partial(attend_kernel, columns),
        grid_spec=pltpu.PrefetchScalarGridSpec(
            num_scalar_prefetch=2,
            grid=(1,),
            in_specs=[
                resident,
                by_rows(depth),
                fixed(bias.shape),
                fixed(cosine.shape),
                fixed(sine.shape),
            ]
            + [by_rows(2 * HD)] * len(keyvals)
            + [resident] * len(pieces),
            out_specs=out_specs,
            scratch_shapes=[
                pltpu.VMEM((rows, width), jnp.bfloat16),
                pltpu.SemaphoreType.DMA((rows // GROUP,)),
            ],
        ),
        out_shape=out_shape[: len(out_specs)],
        compiler_params=pltpu.CompilerParams(vmem_limit_bytes=28 * MIB),
        cost_estimate=matmul_cost(rows, depth, columns.stop - columns.start, 2),
        name="attend",
    )(dest, lengths, total, x, bias, cosine, sine, *keyvals, *pieces)


def place_kernel(source_ref, received_ref, *parts):
    per_part = parts[0].shape[0] // GROUP
    for k, part in enumerate(parts):
        for j in range(per_part):
            part[j * GROUP : (j + 1) * GROUP, :] = received_ref[source_ref[k * per_part + j]]


def place(source, received, parts):
    packs, group, width = received.shape
    per_part = source.shape[0] // parts
    resident = pl.BlockSpec(memory_space=pltpu.VMEM)
    return pl.pallas_call(
        place_kernel,
        grid_spec=pltpu.PrefetchScalarGridSpec(
            num_scalar_prefetch=1,
            grid=(1,),
            in_specs=[resident],
            out_specs=[resident] * parts,
        ),
        out_shape=[jax.ShapeDtypeStruct((per_part * group, width), received.dtype)] * parts,
        compiler_params=pltpu.CompilerParams(vmem_limit_bytes=8 * MIB),
        name="place",
    )(source, received)


def join_kernel(step, start, order_ref, *refs):
    parts, out_ref, sems = refs[:-2], refs[-2], refs[-1]
    if start > 0:
        parts = parts[1:]
    width = parts[0].shape[1]
    copies = []
    for k, part in enumerate(parts):
        column = pl.multiple_of(order_ref[k] * step + start, HD)
        copies.append(
            pltpu.make_async_copy(part, out_ref.at[:, pl.ds(column, width)], sems.at[k])
        )
    for copy in copies:
        copy.start()
    for copy in copies:
        copy.wait()


def join(order, parts, columns, joined=None, start=0):
    rows = parts[0].shape[0]
    whole = pl.BlockSpec(memory_space=pltpu.HBM)
    given = [] if joined is None else [joined]
    return pl.pallas_call(
        functools.partial(join_kernel, columns // len(parts), start),
        grid_spec=pltpu.PrefetchScalarGridSpec(
            num_scalar_prefetch=1,
            grid=(1,),
            in_specs=[whole] * len(given)
            + [pl.BlockSpec(memory_space=pltpu.VMEM)] * len(parts),
            out_specs=whole,
            scratch_shapes=[pltpu.SemaphoreType.DMA((len(parts),))],
        ),
        out_shape=jax.ShapeDtypeStruct((rows, columns), parts[0].dtype),
        input_output_aliases={1: 0} if given else {},
        compiler_params=pltpu.CompilerParams(vmem_limit_bytes=8 * MIB),
        name="join",
    )(order, *given, *parts)


def held_until(value, *others):
    return lax.optimization_barrier((value, *others))[0]


def per_device(
    hidden_states,
    norm_gain,
    w_query,
    w_keyval,
    query_bias,
    keyval_bias,
    group_dest,
    group_offset,
    group_length,
):
    own = lax.axis_index("dp")
    plane = lax.axis_index("mp")
    planes = lax.axis_size("mp")
    packs, groups = group_dest.shape
    rows, features = hidden_states.shape

    def first(piece, by):
        return lax.ppermute(piece, "dp", shift_pairs(by, 0))

    def second(piece, by):
        return lax.ppermute(piece, "dp", shift_pairs(0, by))

    def swap(piece):
        return lax.ppermute(piece, "dp", swap_pairs())

    own_dest = lax.dynamic_index_in_dim(group_dest, own, 0, keepdims=False)
    own_length = lax.dynamic_index_in_dim(group_length, own, 0, keepdims=False)
    slot = group_offset // GROUP
    hits = (group_dest == own)[None] & (
        slot[None] == jnp.arange(groups, dtype=jnp.int32)[:, None, None]
    )
    packs_of = jnp.arange(packs, dtype=jnp.int32)[None, :, None]
    source = jnp.sum(jnp.where(hits, packs_of, 0), (1, 2)).reshape(planes, -1)
    step = jnp.arange(planes, dtype=jnp.int32)
    source = source[(plane + step) % planes].reshape(-1)
    joins = (plane - jnp.array([0, 2, 1, 3], jnp.int32)) % planes
    plan = own_dest, own_length, source, joins

    cut = FIRST_HEADS * HD
    weights = side_by_side(w_query, w_keyval)
    bias = jnp.concatenate([query_bias[:cut], keyval_bias, query_bias[cut:]])[None]
    rows_held = weights.shape[0]
    half = rows_held // 2
    order = lax.dynamic_index_in_dim(jnp.asarray(source_table()), own, 0, keepdims=False)
    widths = [count * rows_held for count in PIECES]
    gain = norm_gain[None]

    near = [first(weights, 1), first(weights, -1), first(weights, 2)]
    near += [second(weights, 1), second(weights, -1)]
    scale, x_near = norm(order, hidden_states, gain, widths[:1])
    near, scale, x_near, plan, bias = lax.optimization_barrier((near, scale, x_near, plan, bias))
    own_dest, own_length, source, joins = plan

    own_ahead, own_behind = near[3:]
    beside = jnp.concatenate(near[:3])
    ahead, behind = second(beside, 1), second(beside, -1)
    x_middle, x_corners, x_swapped, x_far, x_last = norm(
        order, hidden_states, gain, widths[1:], scale, widths[0] // half
    )
    straight = jnp.concatenate([weights, own_ahead, own_behind])
    total = project(None, x_near, [beside, straight])
    pairs = [beside[: 2 * rows_held], jnp.concatenate([near[2], weights]), straight[rows_held:]]
    pairs = [swap(held_until(piece, total)) for piece in pairs]
    total = project(total, x_middle, pairs, SHORT)

    ahead, behind, straight, total, x_corners, x_swapped, x_far, x_last = lax.optimization_barrier(
        (ahead, behind, straight, total, x_corners, x_swapped, x_far, x_last)
    )
    far = [
        second(
            jnp.concatenate(
                [behind[rows_held : 2 * rows_held], behind[-half:], straight[-half:]]
            ),
            -1,
        ),
        second(
            jnp.concatenate(
                [
                    ahead[:rows_held],
                    ahead[2 * rows_held : -half],
                    straight[rows_held : rows_held + half],
                ]
            ),
            1,
        ),
    ]
    total = project(total, x_corners, [ahead, behind])
    total = project(total, x_swapped, [swap(ahead), swap(behind)])
    far, total = lax.optimization_barrier((far, total))
    middle = cut + w_keyval.shape[1]
    last = [swap(piece[:, :middle]) for piece in far]
    total = project(total, x_far, far)

    given = (own_dest, own_length, total, x_last, bias)
    first_sent, keyval = attend(*given, None, last, packs, slice(0, middle))
    last = [swap(held_until(piece[:, middle:], keyval)) for piece in far]
    (second_sent,) = attend(*given, keyval, last, packs, slice(middle, weights.shape[1]))

    def exchanged(sent):
        received = lax.all_to_all(sent, "dp", split_axis=0, concat_axis=0, tiled=True)
        parts = place(source, received, planes)
        return [parts[0]] + [
            lax.ppermute(parts[k], "mp", [(i, (i + k) % planes) for i in range(planes)])
            for k in (2, 1, 3)
        ]

    columns = planes * w_query.shape[1]
    joined = join(joins, exchanged(first_sent), columns)
    return join(joins, exchanged(second_sent), columns, joined, cut)


def solution(mesh):
    return jax.shard_map(
        per_device,
        mesh=mesh,
        in_specs=(
            P("dp", None),
            P(),
            P("dp", "mp"),
            P("dp", "mp"),
            P("mp"),
            P("mp"),
            P(),
            P(),
            P(),
        ),
        out_specs=P(("dp", "mp"), None),
        check_vma=False,
    )
```

```python
import functools

import jax
import jax.numpy as jnp
import numpy as np
from jax import lax
from jax.experimental import pallas as pl
from jax.experimental.pallas import tpu as pltpu
from jax.sharding import PartitionSpec as P

HD = 128
GROUP = 64
SIDE = 4
MIB = 1024 * 1024
FIRST_HEADS = 6
PIECES = (6, 6, 6, 6, 4, 4)

rope_base = 1000000.0
norm_epsilon = 1e-06


def rope_tables():
    half = HD // 2
    frequency = np.float32(rope_base) ** (
        -(np.arange(half, dtype=np.float32) * np.float32(2.0)) / np.float32(HD)
    )
    within = np.arange(GROUP)
    position = np.concatenate([within % length for length in (64, 32, 16, 8)])
    angles = position.astype(np.float32)[:, None] * frequency[None, :].astype(np.float32)
    cosine, sine = np.cos(angles), np.sin(angles)
    return (
        np.concatenate([cosine, cosine], 1).astype(np.float32),
        np.concatenate([-sine, sine], 1).astype(np.float32),
    )


def device_index(y, z, core):
    return ((y % SIDE) * SIDE + (z % SIDE)) * 2 + core


def shift_pairs(first, second):
    pairs = []
    for y in range(SIDE):
        for z in range(SIDE):
            pairs.append((device_index(y, z, 0), device_index(y + first, z + second, 0)))
            pairs.append((device_index(y, z, 1), device_index(y + second, z + first, 1)))
    return pairs


def swap_pairs():
    return [
        (device_index(y, z, core), device_index(y, z, 1 - core))
        for y in range(SIDE)
        for z in range(SIDE)
        for core in range(2)
    ]


def source_table():
    table = np.zeros((32, 64), np.int32)
    for y in range(SIDE):
        for z in range(SIDE):
            for core in range(2):

                def blocks(c, offsets):
                    found = []
                    for a, b, halves in offsets:
                        held = (
                            device_index(y - a, z - b, c)
                            if c == 0
                            else device_index(y - b, z - a, c)
                        )
                        found += [2 * held + half for half in halves]
                    return found

                both, low, high = (0, 1), (0,), (1,)
                near = [(1, 0, both), (3, 0, both), (2, 0, both)]
                near += [(0, 0, both), (0, 1, both), (0, 3, both)]
                corners = [(1, 1, both), (3, 1, both), (2, 1, both)]
                corners += [(1, 3, both), (3, 3, both), (2, 3, both)]
                far = [(3, 2, both), (2, 2, high), (0, 2, high)]
                far += [(1, 2, both), (2, 2, low), (0, 2, low)]
                order = []
                for offsets in (near, corners, far):
                    order += blocks(core, offsets) + blocks(1 - core, offsets)
                table[device_index(y, z, core)] = order
    return table


def beside_kernel(query_ref, keyval_ref, out_ref, sems):
    cut = FIRST_HEADS * HD
    middle = cut + keyval_ref.shape[1]
    copies = [
        pltpu.make_async_copy(
            query_ref.at[:, pl.ds(0, cut)], out_ref.at[:, pl.ds(0, cut)], sems.at[0]
        ),
        pltpu.make_async_copy(
            keyval_ref, out_ref.at[:, pl.ds(cut, middle - cut)], sems.at[1]
        ),
        pltpu.make_async_copy(
            query_ref.at[:, pl.ds(cut, query_ref.shape[1] - cut)],
            out_ref.at[:, pl.ds(middle, out_ref.shape[1] - middle)],
            sems.at[2],
        ),
    ]
    for copy in copies:
        copy.start()
    for copy in copies:
        copy.wait()


def side_by_side(w_query, w_keyval):
    rows = w_query.shape[0]
    return pl.pallas_call(
        beside_kernel,
        in_specs=[pl.BlockSpec(memory_space=pltpu.HBM)] * 2,
        out_specs=pl.BlockSpec(memory_space=pltpu.VMEM),
        out_shape=jax.ShapeDtypeStruct(
            (rows, w_query.shape[1] + w_keyval.shape[1]), w_query.dtype
        ),
        scratch_shapes=[pltpu.SemaphoreType.DMA((3,))],
        compiler_params=pltpu.CompilerParams(vmem_limit_bytes=58 * MIB),
        name="side_by_side",
    )(w_query, w_keyval)


def scaled_columns(order_ref, place, hidden_ref, gain_ref, scale, refs):
    depth = hidden_ref.shape[1] // order_ref.shape[0]
    for ref in refs:
        for j in range(ref.shape[1] // depth):
            start = pl.multiple_of(order_ref[place] * depth, depth)
            block = hidden_ref[:, pl.ds(start, depth)].astype(jnp.float32)
            gain = gain_ref[:, pl.ds(start, depth)]
            ref[:, j * depth : (j + 1) * depth] = (block * scale * gain).astype(jnp.bfloat16)
            place += 1


def norm_kernel(order_ref, hidden_ref, gain_ref, scale_ref, *refs):
    widened = hidden_ref[...].astype(jnp.float32)
    mean_square = jnp.sum(widened * widened, -1, keepdims=True) * (1.0 / widened.shape[1])
    scale = lax.rsqrt(mean_square + norm_epsilon)
    scale_ref[...] = scale
    scaled_columns(order_ref, 0, hidden_ref, gain_ref, scale, refs)


def norm_rest_kernel(place, order_ref, hidden_ref, gain_ref, scale_ref, *refs):
    scaled_columns(order_ref, place, hidden_ref, gain_ref, scale_ref[...], refs)


def norm(order, hidden, gain, widths, scale=None, place=0):
    rows, features = hidden.shape
    tile = 128
    given = [hidden, gain] + ([] if scale is None else [scale])
    in_specs = [
        pl.BlockSpec((tile, features), lambda i, order: (i, 0)),
        pl.BlockSpec((1, features), lambda i, order: (0, 0)),
    ]
    out_specs = [pl.BlockSpec((tile, w), lambda i, order: (i, 0)) for w in widths]
    out_shape = [pltpu.HBM((rows, w), jnp.bfloat16) for w in widths]
    scale_spec = pl.BlockSpec((tile, 1), lambda i, order: (i, 0))
    if scale is None:
        out_specs = [scale_spec] + out_specs
        out_shape = [jax.ShapeDtypeStruct((rows, 1), jnp.float32)] + out_shape
    else:
        in_specs = in_specs + [scale_spec]
    return pl.pallas_call(
        norm_kernel if scale is None else functools.partial(norm_rest_kernel, place),
        grid_spec=pltpu.PrefetchScalarGridSpec(
            num_scalar_prefetch=1, grid=(rows // tile,), in_specs=in_specs, out_specs=out_specs
        ),
        out_shape=out_shape,
        compiler_params=pltpu.CompilerParams(vmem_limit_bytes=18 * MIB),
        cost_estimate=pl.CostEstimate(
            flops=6 * rows * features,
            bytes_accessed=2 * rows * (features + sum(widths)),
            transcendentals=rows,
        ),
        name="norm",
    )(order, *given)


def product(x_ref, pieces):
    weights = jnp.concatenate([piece[...] for piece in pieces], axis=0)
    return jnp.dot(x_ref[...], weights, preferred_element_type=jnp.float32)


def tile_rows(tile):
    return pl.ds(pl.multiple_of(pl.program_id(0) * tile, tile), tile)


def first_kernel(x_ref, *refs):
    refs[-1][tile_rows(x_ref.shape[0]), :] = product(x_ref, refs[:-1])


def add_kernel(total_ref, x_ref, *refs):
    rows = tile_rows(x_ref.shape[0])
    refs[-1][rows, :] = total_ref[rows, :] + product(x_ref, refs[:-1])


def matmul_cost(rows, depth, columns, more):
    return pl.CostEstimate(
        flops=2 * rows * depth * columns,
        bytes_accessed=2 * depth * (rows + columns) + 4 * more * rows * columns,
        transcendentals=0,
    )


SHORT = pl.CostEstimate(flops=1024, bytes_accessed=1024, transcendentals=0)


def project(total, x, pieces, cost=None):
    rows, depth = x.shape
    columns = pieces[0].shape[1]
    tile = 512
    resident = pl.BlockSpec(memory_space=pltpu.VMEM)
    x_block = pl.BlockSpec((tile, depth), lambda i: (i, 0))
    totals = [] if total is None else [total]
    return pl.pallas_call(
        add_kernel if totals else first_kernel,
        grid=(rows // tile,),
        in_specs=[resident] * len(totals) + [x_block] + [resident] * len(pieces),
        out_specs=resident,
        out_shape=jax.ShapeDtypeStruct((rows, columns), jnp.float32),
        input_output_aliases={0: 0} if totals else {},
        compiler_params=pltpu.CompilerParams(vmem_limit_bytes=20 * MIB),
        cost_estimate=cost or matmul_cost(rows, depth, columns, 2),
        name="project",
    )(*totals, x, *pieces)


def attend_kernel(
    columns, dest_ref, length_ref, total_ref, x_ref, bias_ref, cosine_ref, sine_ref, *refs
):
    makes_keyval = columns.start == 0
    if makes_keyval:
        pieces, (out_ref, keyval_ref, context, sems) = refs[:-4], refs[-4:]
    else:
        keyval_ref, pieces, (out_ref, context, sems) = refs[0], refs[1:-3], refs[-3:]
    rows = x_ref.shape[0]
    heads = context.shape[1] // HD
    groups = rows // GROUP

    lengths = [length_ref[g] for g in range(groups)]
    row_tables = []
    for table in (cosine_ref, sine_ref):
        parts = []
        for length in lengths:
            index = (
                (length < 64).astype(jnp.int32)
                + (length < 32).astype(jnp.int32)
                + (length < 16).astype(jnp.int32)
            )
            parts.append(table[pl.ds(pl.multiple_of(index * GROUP, GROUP), GROUP), :])
        row_tables.append(jnp.concatenate(parts, 0))
    cosine, sine = row_tables

    summed = (
        total_ref[:, columns]
        + product(x_ref, pieces)
        + bias_ref[:, columns]
    )

    def rotated(column):
        head = summed[:, column : column + HD]
        return (head * cosine + pltpu.roll(head, HD // 2, 1) * sine).astype(jnp.bfloat16)

    query = [rotated(h * HD) for h in range(heads)]
    if makes_keyval:
        key = rotated(heads * HD)
        value = summed[:, (heads + 1) * HD :].astype(jnp.bfloat16)
        keyval_ref[:, :HD] = key
        keyval_ref[:, HD:] = value
    else:
        key, value = keyval_ref[:, :HD], keyval_ref[:, HD:]

    copies = []
    tile = 2 * GROUP
    row = lax.broadcasted_iota(jnp.int32, (tile, tile), 0)
    column = lax.broadcasted_iota(jnp.int32, (tile, tile), 1)
    for t in range(rows // tile):
        length = jnp.where(row < GROUP, lengths[2 * t], lengths[2 * t + 1])
        allowed = (column >= (row & -length)) & (column <= row)
        span = slice(t * tile, (t + 1) * tile)
        stacked = jnp.concatenate([q[span] for q in query], 0)
        scores = lax.dot_general(
            stacked, key[span], (((1,), (1,)), ((), ())), preferred_element_type=jnp.float32
        ) * (HD ** (-0.5))
        scores = jnp.where(allowed[None], scores.reshape(heads, tile, tile), -jnp.inf)
        weights = jnp.exp(scores - jnp.max(scores, -1, keepdims=True))
        weights = weights * (1.0 / jnp.sum(weights, -1, keepdims=True))
        weights = weights.astype(jnp.bfloat16).reshape(heads * tile, tile)
        mixed = jnp.dot(weights, value[span], preferred_element_type=jnp.float32)
        mixed = mixed.astype(jnp.bfloat16)
        for h in range(heads):
            context[span, h * HD : (h + 1) * HD] = mixed[h * tile : (h + 1) * tile]
        for g in (2 * t, 2 * t + 1):
            copy = pltpu.make_async_copy(
                context.at[pl.ds(g * GROUP, GROUP)], out_ref.at[dest_ref[g]], sems.at[g]
            )
            copy.start()
            copies.append(copy)
    for copy in copies:
        copy.wait()


def attend(dest, lengths, total, x, bias, keyval, pieces, packs, columns):
    rows, depth = x.shape
    cosine, sine = rope_tables()
    resident = pl.BlockSpec(memory_space=pltpu.VMEM)

    def fixed(shape):
        return pl.BlockSpec(
            shape, lambda i, *_: (0,) * len(shape), pipeline_mode=pl.Buffered(1)
        )

    def by_rows(width):
        return pl.BlockSpec((rows, width), lambda i, *_: (i, 0))

    width = columns.stop - columns.start
    out_specs = [pl.BlockSpec(memory_space=pltpu.HBM)]
    if keyval is None:
        width -= 2 * HD
        out_specs.append(by_rows(2 * HD))
    out_shape = [
        pltpu.HBM((packs, GROUP, width), jnp.bfloat16),
        jax.ShapeDtypeStruct((rows, 2 * HD), jnp.bfloat16),
    ]
    keyvals = [] if keyval is None else [keyval]
    return pl.pallas_call(
        functools.partial(attend_kernel, columns),
        grid_spec=pltpu.PrefetchScalarGridSpec(
            num_scalar_prefetch=2,
            grid=(1,),
            in_specs=[
                resident,
                by_rows(depth),
                fixed(bias.shape),
                fixed(cosine.shape),
                fixed(sine.shape),
            ]
            + [by_rows(2 * HD)] * len(keyvals)
            + [resident] * len(pieces),
            out_specs=out_specs,
            scratch_shapes=[
                pltpu.VMEM((rows, width), jnp.bfloat16),
                pltpu.SemaphoreType.DMA((rows // GROUP,)),
            ],
        ),
        out_shape=out_shape[: len(out_specs)],
        compiler_params=pltpu.CompilerParams(vmem_limit_bytes=28 * MIB),
        cost_estimate=matmul_cost(rows, depth, columns.stop - columns.start, 2),
        name="attend",
    )(dest, lengths, total, x, bias, cosine, sine, *keyvals, *pieces)


def place_kernel(source_ref, received_ref, *parts):
    per_part = parts[0].shape[0] // GROUP
    for k, part in enumerate(parts):
        for j in range(per_part):
            part[j * GROUP : (j + 1) * GROUP, :] = received_ref[source_ref[k * per_part + j]]


def place(source, received, parts):
    packs, group, width = received.shape
    per_part = source.shape[0] // parts
    resident = pl.BlockSpec(memory_space=pltpu.VMEM)
    return pl.pallas_call(
        place_kernel,
        grid_spec=pltpu.PrefetchScalarGridSpec(
            num_scalar_prefetch=1,
            grid=(1,),
            in_specs=[resident],
            out_specs=[resident] * parts,
        ),
        out_shape=[jax.ShapeDtypeStruct((per_part * group, width), received.dtype)] * parts,
        compiler_params=pltpu.CompilerParams(vmem_limit_bytes=8 * MIB),
        name="place",
    )(source, received)


def join_kernel(step, start, order_ref, *refs):
    parts, out_ref, sems = refs[:-2], refs[-2], refs[-1]
    if start > 0:
        parts = parts[1:]
    width = parts[0].shape[1]
    copies = []
    for k, part in enumerate(parts):
        column = pl.multiple_of(order_ref[k] * step + start, HD)
        copies.append(
            pltpu.make_async_copy(part, out_ref.at[:, pl.ds(column, width)], sems.at[k])
        )
    for copy in copies:
        copy.start()
    for copy in copies:
        copy.wait()


def join(order, parts, columns, joined=None, start=0):
    rows = parts[0].shape[0]
    whole = pl.BlockSpec(memory_space=pltpu.HBM)
    given = [] if joined is None else [joined]
    return pl.pallas_call(
        functools.partial(join_kernel, columns // len(parts), start),
        grid_spec=pltpu.PrefetchScalarGridSpec(
            num_scalar_prefetch=1,
            grid=(1,),
            in_specs=[whole] * len(given)
            + [pl.BlockSpec(memory_space=pltpu.VMEM)] * len(parts),
            out_specs=whole,
            scratch_shapes=[pltpu.SemaphoreType.DMA((len(parts),))],
        ),
        out_shape=jax.ShapeDtypeStruct((rows, columns), parts[0].dtype),
        input_output_aliases={1: 0} if given else {},
        compiler_params=pltpu.CompilerParams(vmem_limit_bytes=8 * MIB),
        name="join",
    )(order, *given, *parts)


def held_until(value, *others):
    return lax.optimization_barrier((value, *others))[0]


def per_device(
    hidden_states,
    norm_gain,
    w_query,
    w_keyval,
    query_bias,
    keyval_bias,
    group_dest,
    group_offset,
    group_length,
):
    own = lax.axis_index("dp")
    plane = lax.axis_index("mp")
    planes = lax.axis_size("mp")
    packs, groups = group_dest.shape
    rows, features = hidden_states.shape

    def first(piece, by):
        return lax.ppermute(piece, "dp", shift_pairs(by, 0))

    def second(piece, by):
        return lax.ppermute(piece, "dp", shift_pairs(0, by))

    def swap(piece):
        return lax.ppermute(piece, "dp", swap_pairs())

    own_dest = lax.dynamic_index_in_dim(group_dest, own, 0, keepdims=False)
    own_length = lax.dynamic_index_in_dim(group_length, own, 0, keepdims=False)
    slot = group_offset // GROUP
    hits = (group_dest == own)[None] & (
        slot[None] == jnp.arange(groups, dtype=jnp.int32)[:, None, None]
    )
    packs_of = jnp.arange(packs, dtype=jnp.int32)[None, :, None]
    source = jnp.sum(jnp.where(hits, packs_of, 0), (1, 2)).reshape(planes, -1)
    step = jnp.arange(planes, dtype=jnp.int32)
    source = source[(plane + step) % planes].reshape(-1)
    joins = (plane - jnp.array([0, 2, 1, 3], jnp.int32)) % planes
    plan = own_dest, own_length, source, joins

    cut = FIRST_HEADS * HD
    weights = side_by_side(w_query, w_keyval)
    bias = jnp.concatenate([query_bias[:cut], keyval_bias, query_bias[cut:]])[None]
    rows_held = weights.shape[0]
    half = rows_held // 2
    order = lax.dynamic_index_in_dim(jnp.asarray(source_table()), own, 0, keepdims=False)
    widths = [count * rows_held for count in PIECES]
    gain = norm_gain[None]

    near = [first(weights, 1), first(weights, -1), first(weights, 2)]
    near += [second(weights, 1), second(weights, -1)]
    scale, x_near = norm(order, hidden_states, gain, widths[:1])
    near, scale, x_near, plan = lax.optimization_barrier((near, scale, x_near, plan))
    own_dest, own_length, source, joins = plan

    own_ahead, own_behind = near[3:]
    beside = jnp.concatenate(near[:3])
    ahead, behind = second(beside, 1), second(beside, -1)
    x_middle, x_corners, x_swapped, x_far, x_last = norm(
        order, hidden_states, gain, widths[1:], scale, widths[0] // half
    )
    straight = jnp.concatenate([weights, own_ahead, own_behind])
    total = project(None, x_near, [beside, straight])
    pairs = [beside[: 2 * rows_held], jnp.concatenate([near[2], weights]), straight[rows_held:]]
    pairs = [swap(held_until(piece, total)) for piece in pairs]
    total = project(total, x_middle, pairs, SHORT)

    ahead, behind, straight, total, x_corners, x_swapped, x_far, x_last = lax.optimization_barrier(
        (ahead, behind, straight, total, x_corners, x_swapped, x_far, x_last)
    )
    far = [
        second(
            jnp.concatenate(
                [behind[rows_held : 2 * rows_held], behind[-half:], straight[-half:]]
            ),
            -1,
        ),
        second(
            jnp.concatenate(
                [
                    ahead[:rows_held],
                    ahead[2 * rows_held : -half],
                    straight[rows_held : rows_held + half],
                ]
            ),
            1,
        ),
    ]
    total = project(total, x_corners, [ahead, behind])
    total = project(total, x_swapped, [swap(ahead), swap(behind)])
    far, total = lax.optimization_barrier((far, total))
    middle = cut + w_keyval.shape[1]
    last = [swap(piece[:, :middle]) for piece in far]
    total = project(total, x_far, far)

    given = (own_dest, own_length, total, x_last, bias)
    first_sent, keyval = attend(*given, None, last, packs, slice(0, middle))
    last = [swap(held_until(piece[:, middle:], keyval)) for piece in far]
    (second_sent,) = attend(*given, keyval, last, packs, slice(middle, weights.shape[1]))

    def exchanged(sent):
        received = lax.all_to_all(sent, "dp", split_axis=0, concat_axis=0, tiled=True)
        parts = place(source, received, planes)
        return [parts[0]] + [
            lax.ppermute(parts[k], "mp", [(i, (i + k) % planes) for i in range(planes)])
            for k in (2, 1, 3)
        ]

    columns = planes * w_query.shape[1]
    joined = join(joins, exchanged(first_sent), columns)
    return join(joins, exchanged(second_sent), columns, joined, cut)


def solution(mesh):
    return jax.shard_map(
        per_device,
        mesh=mesh,
        in_specs=(
            P("dp", None),
            P(),
            P("dp", "mp"),
            P("dp", "mp"),
            P("mp"),
            P("mp"),
            P(),
            P(),
            P(),
        ),
        out_specs=P(("dp", "mp"), None),
        check_vma=False,
    )
```
